512 devices in a mesh: dp: 16 (over x, y), expert: 32 (over z, core).
Axes of the slice: x: 4, y: 4, z: 16, core: 2. Of those that a mesh axis runs over, the one named last changes fastest.
Arguments:
- tokens: bfloat16 [1024, 2048], P('dp'), may hold values from -6 to 6
- d_mixed: bfloat16 [1024, 2048], P('dp'), may hold values from -6 to 6
- route_ids: int32 [1024, 6], replicated, may hold values from 0 to 63, all different within a row; in each aligned block of 64 rows (0 to 63, 64 to 127, ...) at most 30 rows name the same one
- route_weight: float32 [1024, 6], replicated, may hold values from 0.05 to 1
- gate_weight: bfloat16 [512, 176, 2048], P(('expert', 'dp')), may hold values from -0.125 to 0.125
- up_weight: bfloat16 [512, 176, 2048], P(('expert', 'dp')), may hold values from -0.125 to 0.125
- down_weight: bfloat16 [512, 176, 2048], P(('expert', 'dp')), may hold values from -0.15625 to 0.15625
Outputs:
- mixed: bfloat16 [1024, 2048], P('dp')
- d_route: float32 [1024, 6], P('dp')
- d_tokens: bfloat16 [1024, 2048], P('dp')
- grad_gate: bfloat16 [512, 176, 2048], P(('expert', 'dp'))
- grad_up: bfloat16 [512, 176, 2048], P(('expert', 'dp'))
- grad_down: bfloat16 [512, 176, 2048], P(('expert', 'dp'))
The draws below stay inside these ranges and needn't reach their ends.
Inputs may be any that keep to these rules, and one draw needn't show every extreme that they name: `route_ids`: each row names 6 different experts. In each aligned block of 64 rows (the tokens of one index of dp) no expert is named by more than 30 rows, and in every draw some expert is named by exactly 30 rows of some block.
All inputs are finite; a program needn't handle non-finite values.
Results may differ from the reference program's by a relative error of at most 0.0064.
Values may be sent and summed in bfloat16 or wider, within the bound.
No kernel may reach another device: no remote copies, remote signals or barrier semaphores. Data moves between devices by JAX's collectives and lax.ppermute only.
A program may use at most 64 MiB of HBM per device.

```python
import math
import jax
import jax.numpy as jnp
import numpy as np
from jax import lax

D = 2048
FF = 1408
TOP = 6
TOK_DEV = 64
EXPERTS = 64
PIECES = 8
HID = 176
TOKENS = 1024
CAP = 30
N_DP = 16


def block_scale(stream_key, extent, cuts, low, high):
    def one(dim, shards_of):
        draws = jax.random.uniform(jax.random.fold_in(jax.random.fold_in(stream_key, 6), dim), (shards_of,), jnp.float32, low / len(cuts), high / len(cuts))
        return jnp.repeat(jnp.exp(draws), extent[dim] // shards_of).reshape((-1,) + (1,) * (len(extent) - dim - 1))

    gain = one(*cuts[0])
    for cut in cuts[1:]:
        gain = gain * one(*cut)
    return gain


def routed_block(key, own, number, rows, amount, top, reach, slope):
    sequence = jax.random.permutation(key, amount)
    heavy_load, common = portions_of(amount, rows * top, reach, slope, True), portions_of(amount, rows * top, reach, slope, False)
    places = jnp.arange(amount)

    def named(tallies, rotation):
        used = int((tallies > 0).sum())
        fixed = max(1, used // 4)
        passed = fixed + (places - fixed + rotation * (used - fixed)) % max(1, amount - fixed)
        return jnp.zeros((amount,), jnp.int32).at[sequence[jnp.where(places < fixed, places, passed)]].set(jnp.asarray(tallies, jnp.int32))

    tallies = jnp.where(number % 4 == 0, named(heavy_load, number // 4), named(common, number - number // 4 - 1))
    mixed = jax.random.permutation(jax.random.fold_in(own, 3), amount)
    donor, receiver = mixed[0:amount // 2 * 2:2], mixed[1:amount // 2 * 2:2]
    slack = jnp.minimum(tallies[donor] - 1, reach - tallies[receiver]) // 2
    slack = jnp.where((donor == sequence[0]) | (receiver == sequence[0]) | (tallies[receiver] == 0), 0, jnp.maximum(slack, 0))
    passed = jax.random.randint(jax.random.fold_in(own, 4), (amount // 2,), 0, 1 << 20) % (slack + 1)
    tallies = tallies.at[donor].add(-passed).at[receiver].add(passed)
    members = jnp.searchsorted(jnp.cumsum(tallies), jnp.arange(rows * top), side="right").astype(jnp.int32)
    listing = members.reshape(top, rows).T
    listing = listing[jax.random.permutation(jax.random.fold_in(own, 1), rows)]
    rotation = jax.random.randint(jax.random.fold_in(own, 2), (rows, 1), 0, top)
    return jnp.take_along_axis(listing, (jnp.arange(top)[None, :] + rotation) % top, axis=1)


def portions_of(amount, total, reach, skew, full):
    portions = [(1 << 20) // math.isqrt(grade ** skew) + 1 for grade in range(1, amount + 1)]
    largest = reach if full else min(reach, max(-(-total // amount), total * portions[0] // sum(portions)))
    least = 1 if total - largest >= amount - 1 else 0
    holding, rest = [largest] + [least] * (amount - 1), total - largest - least * (amount - 1)
    while rest > 0:
        candidates = [i for i in range(1, amount) if holding[i] < largest] or [i for i in range(1, amount) if holding[i] < reach]
        pool, remaining = sum([portions[i] for i in candidates]), rest
        for i in candidates:
            addition = min(reach - holding[i], max(1, remaining * portions[i] // pool), rest)
            holding[i] = holding[i] + addition
            rest = rest - addition
    return np.array(holding)


def bell_draw(key, dims, width, bound, pieces=(), kind=jnp.bfloat16):
    factor_of = block_scale(key, dims, pieces, -0.22, 0.18) if pieces else 1.0
    entries = jax.random.normal(key, dims, jnp.float32) * width * factor_of
    return jnp.minimum(jnp.maximum(entries, -bound), bound).astype(kind)


def setup_inputs(seed: int = 0) -> dict:
    seeds = jax.random.split(jax.random.key(seed), 8)
    tokens = bell_draw(seeds[0], (TOKENS, D), 1.0, 6.0, ((0, 16),))
    d_mixed = bell_draw(seeds[1], (TOKENS, D), 1.0, 6.0, ((0, 16),))
    route_ids_keys = jax.random.split(jax.random.fold_in(seeds[2], 1), TOKENS // TOK_DEV)
    route_ids_turns = jax.random.permutation(jax.random.fold_in(seeds[2], 3), TOKENS // TOK_DEV)
    route_ids = jax.vmap(lambda own, number: routed_block(jax.random.fold_in(seeds[2], 2), own, number, TOK_DEV, EXPERTS, TOP, CAP, 2))(route_ids_keys, route_ids_turns).reshape((TOKENS, TOP))
    route_weight = jnp.clip(jax.random.uniform(seeds[3], (TOKENS, TOP), jnp.float32, 0.05, 1.0), 0.05, 1.0)
    gate_weight = bell_draw(seeds[4], (EXPERTS * PIECES, HID, D), D ** -0.5, 0.125, ((0, 512),))
    up_weight = bell_draw(seeds[5], (EXPERTS * PIECES, HID, D), D ** -0.5, 0.125, ((0, 512),))
    down_weight = bell_draw(seeds[6], (EXPERTS * PIECES, HID, D), FF ** -0.5, 0.15625, ((0, 512),))
    return dict(tokens=tokens, d_mixed=d_mixed, route_ids=route_ids, route_weight=route_weight, gate_weight=gate_weight, up_weight=up_weight, down_weight=down_weight)


def slot_table(block_ids, expert_count):
    flat_ids = block_ids.reshape(-1)
    one_hot = (flat_ids[:, None] == jnp.arange(expert_count, dtype=jnp.int32)[None, :]).astype(jnp.int32)
    earlier = jnp.cumsum(one_hot, axis=0) - one_hot
    return jnp.sum(earlier * one_hot, axis=1).astype(jnp.int32)


def block_slots(block_ids):
    return slot_table(block_ids, EXPERTS)


def piece_pass(rows_in, rows_grad, gate_piece, up_piece, down_piece):
    gate_value = jnp.dot(rows_in, gate_piece.T, preferred_element_type=jnp.float32)
    up_value = jnp.dot(rows_in, up_piece.T, preferred_element_type=jnp.float32)
    sigmoid_gate = jax.nn.sigmoid(gate_value)
    activated = gate_value * sigmoid_gate
    hidden = (activated * up_value).astype(jnp.bfloat16)
    part_out = jnp.dot(hidden, down_piece, preferred_element_type=jnp.float32).astype(jnp.bfloat16)
    d_hidden = jnp.dot(rows_grad, down_piece.T, preferred_element_type=jnp.float32)
    grad_down = jnp.dot(hidden.T, rows_grad, preferred_element_type=jnp.float32).astype(jnp.bfloat16)
    d_gate_pre = (d_hidden * up_value * sigmoid_gate * (1.0 + gate_value * (1.0 - sigmoid_gate))).astype(jnp.bfloat16)
    d_up_pre = (d_hidden * activated).astype(jnp.bfloat16)
    grad_gate = jnp.dot(d_gate_pre.T, rows_in, preferred_element_type=jnp.float32).astype(jnp.bfloat16)
    grad_up = jnp.dot(d_up_pre.T, rows_in, preferred_element_type=jnp.float32).astype(jnp.bfloat16)
    part_in = (jnp.dot(d_gate_pre, gate_piece, preferred_element_type=jnp.float32)
               + jnp.dot(d_up_pre, up_piece, preferred_element_type=jnp.float32)).astype(jnp.bfloat16)
    return part_out, part_in, grad_gate, grad_up, grad_down


def expert_pass(packed):
    routed_in, routed_grad, gate_expert, up_expert, down_expert = packed
    rows_in = routed_in.reshape(N_DP * CAP, D)
    rows_grad = routed_grad.reshape(N_DP * CAP, D)
    total_out = jnp.zeros((N_DP * CAP, D), jnp.float32)
    total_in = jnp.zeros((N_DP * CAP, D), jnp.float32)
    gate_grads = []
    up_grads = []
    down_grads = []
    for position in range(PIECES):
        results = piece_pass(rows_in, rows_grad, gate_expert[position], up_expert[position], down_expert[position])
        total_out = total_out + results[0].astype(jnp.float32)
        total_in = total_in + results[1].astype(jnp.float32)
        gate_grads.append(results[2])
        up_grads.append(results[3])
        down_grads.append(results[4])
    return total_out, total_in, jnp.stack(gate_grads), jnp.stack(up_grads), jnp.stack(down_grads)


def reference(tokens, d_mixed, route_ids, route_weight, gate_weight, up_weight, down_weight):
    blocks = route_ids.reshape(N_DP, TOK_DEV, TOP)
    slot_numbers = jax.vmap(block_slots)(blocks).reshape(-1)
    flat_ids = route_ids.reshape(-1).astype(jnp.int32)
    flat_tokens = jnp.arange(TOKENS * TOP, dtype=jnp.int32) // TOP
    flat_blocks = flat_tokens // TOK_DEV
    flat_weight = route_weight.reshape(-1)
    routed_in = jnp.zeros((EXPERTS, N_DP, CAP, D), jnp.bfloat16)
    routed_in = routed_in.at[flat_ids, flat_blocks, slot_numbers].set(tokens[flat_tokens])
    grad_rows = (flat_weight[:, None] * d_mixed[flat_tokens].astype(jnp.float32)).astype(jnp.bfloat16)
    routed_grad = jnp.zeros((EXPERTS, N_DP, CAP, D), jnp.bfloat16)
    routed_grad = routed_grad.at[flat_ids, flat_blocks, slot_numbers].set(grad_rows)
    gate_all = gate_weight.reshape(EXPERTS, PIECES, HID, D)
    up_all = up_weight.reshape(EXPERTS, PIECES, HID, D)
    down_all = down_weight.reshape(EXPERTS, PIECES, HID, D)
    expert_out, expert_in, grad_gate, grad_up, grad_down = lax.map(
        expert_pass, (routed_in, routed_grad, gate_all, up_all, down_all))
    expert_out = expert_out.reshape(EXPERTS, N_DP, CAP, D)
    expert_in = expert_in.reshape(EXPERTS, N_DP, CAP, D)
    picked_out = expert_out[flat_ids, flat_blocks, slot_numbers].reshape(TOKENS, TOP, D)
    picked_in = expert_in[flat_ids, flat_blocks, slot_numbers].reshape(TOKENS, TOP, D)
    mixed = jnp.sum(route_weight[:, :, None] * picked_out, axis=1).astype(jnp.bfloat16)
    d_route = jnp.sum(picked_out * d_mixed.astype(jnp.float32)[:, None, :], axis=2)
    d_tokens = jnp.sum(picked_in, axis=1).astype(jnp.bfloat16)
    return (mixed, d_route, d_tokens,
            grad_gate.reshape(EXPERTS * PIECES, HID, D),
            grad_up.reshape(EXPERTS * PIECES, HID, D),
            grad_down.reshape(EXPERTS * PIECES, HID, D))
```

```python
import jax
import jax.numpy as jnp
from jax import lax
from jax.experimental import pallas as pl
from jax.experimental.pallas import tpu as pltpu
from jax.sharding import Mesh, PartitionSpec as P

CORES = 2
EXP_DEV = 2
SLOTS = 32
LANES = 128
BF = jnp.bfloat16
F32 = jnp.float32


def dot(left, right, left_dim=1, right_dim=0):
    return lax.dot_general(
        left, right, (((left_dim,), (right_dim,)), ((), ())), preferred_element_type=F32
    )


def iota(shape, dim):
    return lax.broadcasted_iota(jnp.int32, shape, dim)


def earlier_rows(count):
    return (iota((count, count), 1) < iota((count, count), 0)).astype(BF)


def named(ids, lane_expert):
    hit = ids[:, 0:1] == lane_expert
    for k in range(1, ids.shape[1]):
        hit = jnp.logical_or(hit, ids[:, k : k + 1] == lane_expert)
    return hit


def named_weight(ids, weight, lane_expert):
    total = jnp.where(ids[:, 0:1] == lane_expert, weight[:, 0:1], 0.0)
    for k in range(1, ids.shape[1]):
        total = total + jnp.where(ids[:, k : k + 1] == lane_expert, weight[:, k : k + 1], 0.0)
    return total


def placed(hit, slot_lane):
    flag = hit.astype(F32)
    slot = dot(earlier_rows(hit.shape[0]), flag.astype(BF))
    return jnp.where(slot == slot_lane.astype(F32), flag, 0.0)


def split(value):
    high = value.astype(BF)
    return high, (value - high.astype(F32)).astype(BF)


def call(kernel, outs, scalars, *arrays, scratch=()):
    vmem = pl.BlockSpec(memory_space=pltpu.VMEM)
    return pl.pallas_call(
        kernel,
        out_shape=[jax.ShapeDtypeStruct(shape, kind) for shape, kind in outs],
        in_specs=[pl.BlockSpec(memory_space=pltpu.SMEM)] + [vmem] * len(arrays),
        out_specs=[vmem] * len(outs),
        scratch_shapes=list(scratch),
        compiler_params=pltpu.CompilerParams(vmem_limit_bytes=48 << 20),
    )(jnp.stack(scalars).astype(jnp.int32), *arrays)


def send_kernel(where, ids, tokens, out):
    first_expert = where[0]
    dp_count = out.shape[0]
    rows = tokens.shape[0]
    lane = iota((rows, EXP_DEV * SLOTS), 1)
    hit = named(ids[...], first_expert + lane // SLOTS)
    pick = placed(hit, lane % SLOTS).astype(BF)
    picked = dot(pick, tokens[...], 0, 0).astype(BF)
    for d in range(dp_count):
        j = d // (dp_count // EXP_DEV)
        out[d] = picked[j * SLOTS : (j + 1) * SLOTS]


def table_kernel(where, ids, weight, place, scale):
    expert = where[0]
    block = where_rows = 64
    total = ids.shape[0]
    lane = iota((block, SLOTS), 1)
    scale[...] = named_weight(ids[...], weight[...], jnp.full((total, 1), expert, jnp.int32))
    for b in range(total // block):
        part = ids[b * block : (b + 1) * block, :]
        hit = named(part, jnp.full((block, SLOTS), expert, jnp.int32))
        place[b * block : (b + 1) * block, :] = placed(hit, lane).astype(BF)


def forward_kernel(where, rows_in, gate_w, up_w, down_w, out, gate, up, hidden):
    x = rows_in[...]
    g = dot(x, gate_w[...], 1, 1)
    u = dot(x, up_w[...], 1, 1)
    gate[...] = g
    up[...] = u
    h = (g * jax.nn.sigmoid(g) * u).astype(BF)
    hidden[...] = h
    half = out.shape[2]
    for c in range(CORES):
        piece = dot(h, down_w[:, c * half : (c + 1) * half]).astype(BF)
        for d in range(out.shape[0] // CORES):
            out[CORES * d + c] = piece[d * SLOTS : (d + 1) * SLOTS]


def backward_kernel(
    where, d_mixed, place, scale, gate, up, gate_w, up_w, down_w, out, d_gate, d_up, d_hidden
):
    block = 64
    tall = dot(d_mixed[...], down_w[...], 1, 1) * scale[...]
    for b in range(tall.shape[0] // block):
        high, low = split(tall[b * block : (b + 1) * block])
        pick = place[b * block : (b + 1) * block, :]
        d_hidden[b * SLOTS : (b + 1) * SLOTS, :] = dot(pick, high, 0, 0) + dot(pick, low, 0, 0)
    dh = d_hidden[...]
    g = gate[...]
    sig = jax.nn.sigmoid(g)
    dg = (dh * up[...] * sig * (1.0 + g * (1.0 - sig))).astype(BF)
    du = (dh * (g * sig)).astype(BF)
    d_gate[...] = dg
    d_up[...] = du
    half = out.shape[2]
    for c in range(CORES):
        cols = slice(c * half, (c + 1) * half)
        piece = (dot(dg, gate_w[:, cols]) + dot(du, up_w[:, cols])).astype(BF)
        for d in range(out.shape[0] // CORES):
            out[CORES * d + c] = piece[d * SLOTS : (d + 1) * SLOTS]


def grads_kernel(
    where, rows_in, d_mixed, place, scale, hidden, d_gate, d_up, g_gate, g_up, g_down, spread
):
    block = 64
    for b in range(d_mixed.shape[0] // block):
        part = dot(place[b * block : (b + 1) * block, :], hidden[b * SLOTS : (b + 1) * SLOTS, :])
        spread[b * block : (b + 1) * block, :] = (
            part * scale[b * block : (b + 1) * block, :]
        ).astype(BF)
    g_down[...] = dot(spread[...], d_mixed[...], 0, 0).astype(BF)
    g_gate[...] = dot(d_gate[...], rows_in[...], 0, 0).astype(BF)
    g_up[...] = dot(d_up[...], rows_in[...], 0, 0).astype(BF)


def combine_kernel(where, returned, ids, weight, d_mixed, mixed, route, place):
    first_expert, core = where[0], where[1]
    rows = ids.shape[0]
    count, half = returned.shape
    lane = iota((rows, count), 1)
    source = lane // SLOTS
    sources_per_expert = count // SLOTS // EXP_DEV
    expert = first_expert + (source % CORES) * EXP_DEV + source // sources_per_expert
    all_ids = ids[...]
    pick = placed(named(all_ids, expert), lane % SLOTS)
    place[...] = pick.astype(BF)
    weighted = pick * named_weight(all_ids, weight[...], expert)
    high, low = split(weighted)
    back = returned[...]
    mixed[...] = dot(high, back) + dot(low, back)
    own_grad = d_mixed[:, pl.ds(pl.multiple_of(core * half, LANES), half)]
    paired = dot(own_grad, back, 1, 1) * pick
    spot = iota((rows, LANES), 1)
    result = jnp.zeros((rows, LANES), F32)
    for k in range(ids.shape[1]):
        mine = jnp.where(all_ids[:, k : k + 1] == expert, paired, 0.0)
        result = jnp.where(spot % 8 == k, jnp.sum(mine, axis=1, keepdims=True), result)
    route[...] = result


def pack_kernel(where, returned, place, mixed, route, out):
    back = dot(place[...], returned[...])
    high, low = split(route[...])
    half = returned.shape[1]
    for i in range(out.shape[0] // 2):
        rows = slice(8 * i, 8 * i + 8)
        out[2 * i, :, :half] = mixed[rows, :].astype(BF)
        out[2 * i, :, half:] = high.astype(F32)[rows].astype(BF)
        out[2 * i + 1, :, :half] = back[rows].astype(BF)
        out[2 * i + 1, :, half:] = low.astype(F32)[rows].astype(BF)


def total_kernel(where, parts, out):
    total = parts[0].astype(F32)
    for i in range(1, parts.shape[0]):
        total = total + parts[i].astype(F32)
    width = total.shape[1] - LANES
    tail = total[:, width:]
    high, low = split(tail)
    spot = iota(tail.shape, 1)
    tail = jnp.where(spot < 8, high.astype(F32), low.astype(F32)).astype(BF)
    body_part = total[:, :width].astype(BF)
    for i in range(out.shape[0]):
        out[i, :, :width] = body_part
        out[i, :, width:] = tail


def finish_kernel(where, own, other, mixed, d_tokens, route):
    core = where[0]
    width = own.shape[2] - LANES
    for source, side in ((own, core), (other, 1 - core)):
        cols = pl.ds(pl.multiple_of(side * width, LANES), width)
        for target, odd in ((mixed, 0), (d_tokens, 1)):
            for i in range(0, own.shape[0] // 2, 2):
                pair = [source[2 * (i + j) + odd, :, :width].astype(F32) for j in range(2)]
                target[8 * i : 8 * i + 16, cols] = jnp.concatenate(pair, axis=0).astype(BF)
    for i in range(own.shape[0] // 2):
        total = jnp.zeros((8, LANES), F32)
        for source in (own, other):
            for odd in range(2):
                total = total + source[2 * i + odd, :, width:].astype(F32)
        count = route.shape[1]
        route[8 * i : 8 * i + 8, :] = total[:, :count] + total[:, 8 : 8 + count]


def body(tokens, d_mixed, route_ids, route_weight, gate_weight, up_weight, down_weight):
    dp_count = lax.axis_size("dp")
    z_count = lax.axis_size("z")
    dp_index, z_index, core = lax.axis_index("dp"), lax.axis_index("z"), lax.axis_index("core")
    row_count, width = tokens.shape
    half = width // CORES
    hidden_count = gate_weight.shape[1]
    total = dp_count * row_count
    slot_rows = dp_count * SLOTS
    chip_expert = z_index * CORES * EXP_DEV
    column_expert = chip_expert + core * EXP_DEV
    expert = column_expert + dp_index // (dp_count // EXP_DEV)
    gate_piece, up_piece, down_piece = gate_weight[0], up_weight[0], down_weight[0]
    own_ids = lax.dynamic_slice_in_dim(route_ids, dp_index * row_count, row_count, 0)
    own_weight = lax.dynamic_slice_in_dim(route_weight, dp_index * row_count, row_count, 0)

    all_grad = lax.all_gather(d_mixed, "dp", axis=0, tiled=True)

    (sent,) = call(
        send_kernel, [((dp_count, SLOTS, width), BF)], [column_expert], own_ids, tokens
    )
    route_ids, route_weight, own_weight, sent = lax.optimization_barrier(
        (route_ids, route_weight, own_weight, sent)
    )
    rows_in = lax.all_to_all(sent, "dp", 0, 0, tiled=True).reshape(slot_rows, width)
    place, scale = call(
        table_kernel,
        [((total, SLOTS), BF), ((total, 1), F32)],
        [expert],
        route_ids,
        route_weight,
    )

    out, gate, up, hidden = call(
        forward_kernel,
        [
            ((CORES * dp_count, SLOTS, half), BF),
            ((slot_rows, hidden_count), F32),
            ((slot_rows, hidden_count), F32),
            ((slot_rows, hidden_count), BF),
        ],
        [expert],
        rows_in,
        gate_piece,
        up_piece,
        down_piece,
    )
    returned = lax.all_to_all(out, ("dp", "core"), 0, 0, tiled=True)

    out_in, d_gate, d_up = call(
        backward_kernel,
        [
            ((CORES * dp_count, SLOTS, half), BF),
            ((slot_rows, hidden_count), BF),
            ((slot_rows, hidden_count), BF),
        ],
        [expert],
        all_grad,
        place,
        scale,
        gate,
        up,
        gate_piece,
        up_piece,
        down_piece,
        scratch=[pltpu.VMEM((slot_rows, hidden_count), F32)],
    )
    out_in, d_gate, returned = lax.optimization_barrier((out_in, d_gate, returned))
    returned_in = lax.all_to_all(out_in, ("dp", "core"), 0, 0, tiled=True)
    grad_gate, grad_up, grad_down = call(
        grads_kernel,
        [((hidden_count, width), BF)] * 3,
        [expert],
        rows_in,
        all_grad,
        place,
        scale,
        hidden,
        d_gate,
        d_up,
        scratch=[pltpu.VMEM((total, hidden_count), BF)],
    )
    mixed_part, route_part, own_place = call(
        combine_kernel,
        [
            ((row_count, half), F32),
            ((row_count, LANES), F32),
            ((row_count, CORES * slot_rows), BF),
        ],
        [chip_expert, core],
        returned.reshape(CORES * slot_rows, half),
        own_ids,
        own_weight,
        d_mixed,
    )
    (packed,) = call(
        pack_kernel,
        [((z_count, 8, half + LANES), BF)],
        [core],
        returned_in.reshape(CORES * slot_rows, half),
        own_place,
        mixed_part,
        route_part,
    )
    parts = lax.all_to_all(packed, "z", 0, 0, tiled=True)
    (summed,) = call(total_kernel, [((z_count, 8, half + LANES), BF)], [core], parts)
    whole = lax.all_to_all(summed, "z", 0, 0, tiled=True)
    other = lax.ppermute(whole, "core", [(0, 1), (1, 0)])
    mixed, d_tokens, d_route = call(
        finish_kernel,
        [
            ((row_count, width), BF),
            ((row_count, width), BF),
            ((row_count, route_ids.shape[1]), F32),
        ],
        [core],
        whole,
        other,
    )
    return (mixed, d_route, d_tokens, grad_gate[None], grad_up[None], grad_down[None])


def solution(mesh):
    dp_count, expert_count = mesh.devices.shape
    fine = Mesh(
        mesh.devices.reshape(dp_count, expert_count // CORES, CORES), ("dp", "z", "core")
    )
    rows = P("dp", None)
    blocks = P(("z", "core", "dp"), None, None)
    in_specs = (rows, rows, P(), P(), blocks, blocks, blocks)
    out_specs = (rows, rows, rows, blocks, blocks, blocks)
    return jax.shard_map(body, mesh=fine, in_specs=in_specs, out_specs=out_specs, check_vma=False)
```

```python
import jax
import jax.numpy as jnp
from jax import lax
from jax.experimental import pallas as pl
from jax.experimental.pallas import tpu as pltpu
from jax.sharding import Mesh, PartitionSpec as P

CORES = 2
EXP_DEV = 2
SLOTS = 32
LANES = 128
BF = jnp.bfloat16
F32 = jnp.float32


def dot(left, right, left_dim=1, right_dim=0):
    return lax.dot_general(
        left, right, (((left_dim,), (right_dim,)), ((), ())), preferred_element_type=F32
    )


def iota(shape, dim):
    return lax.broadcasted_iota(jnp.int32, shape, dim)


def split(value):
    high = value.astype(BF)
    return high, (value - high.astype(F32)).astype(BF)


def slot_rows_of(ids, expert, slot):
    count = ids.shape[1]
    hit = ids[0:1, :] == expert
    for k in range(1, ids.shape[0]):
        hit = jnp.logical_or(hit, ids[k : k + 1, :] == expert)
    flag = hit.astype(F32)
    earlier = (iota((count, count), 0) < iota((count, count), 1)).astype(BF)
    return jnp.where(dot(flag.astype(BF), earlier) == slot.astype(F32), flag, 0.0)


def rows_of_slots(ids, expert, slot):
    count = ids.shape[0]
    hit = ids[:, 0:1] == expert
    for k in range(1, ids.shape[1]):
        hit = jnp.logical_or(hit, ids[:, k : k + 1] == expert)
    flag = hit.astype(F32)
    earlier = (iota((count, count), 1) < iota((count, count), 0)).astype(BF)
    return jnp.where(dot(earlier, flag.astype(BF)) == slot.astype(F32), flag, 0.0)


VMEM = pl.BlockSpec(memory_space=pltpu.VMEM)
ANY = pl.BlockSpec(memory_space=pl.ANY)


def call(kernel, outs, scalars, arrays, scratch=()):
    return pl.pallas_call(
        kernel,
        out_shape=[jax.ShapeDtypeStruct(shape, kind) for shape, kind, _ in outs],
        in_specs=[pl.BlockSpec(memory_space=pltpu.SMEM)] + [space for _, space in arrays],
        out_specs=[space for _, _, space in outs],
        scratch_shapes=list(scratch),
        compiler_params=pltpu.CompilerParams(vmem_limit_bytes=48 << 20),
    )(jnp.stack(scalars).astype(jnp.int32), *[array for array, _ in arrays])


def begin(pairs, sems):
    copies = [pltpu.make_async_copy(a, b, sems.at[i]) for i, (a, b) in enumerate(pairs)]
    for copy in copies:
        copy.start()
    return copies


def send_kernel(where, ids, tokens, out, held, picked, in_sem, out_sem):
    (load,) = begin([(tokens, held)], in_sem)
    spot = iota((EXP_DEV * SLOTS, 1), 0)
    pick = slot_rows_of(ids[...], where[0] + spot // SLOTS, spot % SLOTS).astype(BF)
    load.wait()
    picked[...] = dot(pick, held[...]).astype(BF).reshape(picked.shape)
    per_expert = out.shape[0] // EXP_DEV
    for copy in begin([(picked.at[d // per_expert], out.at[d]) for d in range(out.shape[0])], out_sem):
        copy.wait()


def forward_kernel(
    where, rows_in, gate_w, up_w, down_w, out, x, gate_v, up_v, down_v, y, in_sem, out_sem
):
    parts = 2
    blocks = x.shape[0] // parts
    loads = begin(
        [(gate_w, gate_v), (rows_in.at[:blocks], x.at[:blocks]), (up_w, up_v), (down_w, down_v)]
        + [(rows_in.at[blocks:], x.at[blocks:])],
        in_sem,
    )
    stores = []
    half = y.shape[3]
    for p in range(parts):
        span = slice(p * blocks, (p + 1) * blocks)
        if p == 0:
            loads[0].wait()
            loads[1].wait()
        else:
            loads[4].wait()
        rows = x[span].reshape(blocks * SLOTS, x.shape[2])
        g = dot(rows, gate_v[...], 1, 1)
        if p == 0:
            loads[2].wait()
        u = dot(rows, up_v[...], 1, 1)
        h = (g * jax.nn.sigmoid(g) * u).astype(BF)
        if p == 0:
            loads[3].wait()
        for c in range(CORES):
            piece = dot(h, down_v[:, c * half : (c + 1) * half]).astype(BF)
            y[c, span] = piece.reshape(blocks, SLOTS, half)
            i = CORES * p + c
            store = pltpu.make_async_copy(y.at[c, span], out.at[span, c], out_sem.at[i])
            store.start()
            stores.append(store)
    for store in stores:
        store.wait()


def factors_kernel(
    where, rows_in, gate_w, up_w, ids, weight, place, gate_factor, up_factor, hidden
):
    expert = where[0]
    block = 64
    x = rows_in[...]
    g = dot(x, gate_w[...], 1, 1)
    u = dot(x, up_w[...], 1, 1)
    sig = jax.nn.sigmoid(g)
    act = g * sig
    gate_factor[...] = u * sig * (1.0 + g * (1.0 - sig))
    up_factor[...] = act
    hidden[...] = (act * u).astype(BF)
    slot = iota((SLOTS, 1), 0)
    for b in range(ids.shape[1] // block):
        cols, rows = slice(b * block, (b + 1) * block), slice(b * SLOTS, (b + 1) * SLOTS)
        part = ids[:, cols]
        pick = slot_rows_of(part, jnp.full((SLOTS, 1), expert, jnp.int32), slot)
        place[rows, :] = pick.astype(BF)
        scale = jnp.zeros((1, block), F32)
        for k in range(part.shape[0]):
            scale = scale + jnp.where(part[k : k + 1, :] == expert, weight[k : k + 1, cols], 0.0)
        scale = jnp.sum(pick * scale, axis=1, keepdims=True)
        gate_factor[rows, :] = gate_factor[rows, :] * scale
        up_factor[rows, :] = up_factor[rows, :] * scale
        hidden[rows, :] = (hidden[rows, :].astype(F32) * scale).astype(BF)


def backward_kernel(
    where, d_mixed, place, gate_factor, up_factor, gate_w, up_w, down_w, out, d_gate, d_up,
    grad_v, place_v, gate_f, up_f, gate_v, up_v, down_v, tall, y, in_sem, out_sem
):
    parts = 2
    block = 64
    half = y.shape[3]
    blocks = y.shape[1] // parts
    near, far = slice(0, blocks), slice(blocks, 2 * blocks)
    loads = begin(
        [
            (down_w, down_v),
            (d_mixed.at[near], grad_v.at[near]),
            (place, place_v),
            (d_mixed.at[far], grad_v.at[far]),
            (gate_factor, gate_f),
            (up_factor, up_f),
            (gate_w, gate_v),
            (up_w, up_v),
        ],
        in_sem,
    )
    stores = []
    for p, span in enumerate((near, far)):
        if p == 0:
            loads[0].wait()
            loads[1].wait()
        else:
            loads[3].wait()
        high = jnp.zeros((blocks * block, down_v.shape[0]), F32)
        for c in range(CORES):
            part = grad_v[span, c].reshape(blocks * block, half)
            high = high + dot(part, down_v[:, c * half : (c + 1) * half], 1, 1)
        high, low = split(high)
        if p == 0:
            loads[2].wait()
        for i in range(blocks):
            b = p * blocks + i
            pick = place_v[b * SLOTS : (b + 1) * SLOTS, :]
            rows = slice(i * block, (i + 1) * block)
            tall[b * SLOTS : (b + 1) * SLOTS, :] = dot(pick, high[rows]) + dot(pick, low[rows])
        if p == 0:
            for load in loads[4:]:
                load.wait()
        rows = slice(p * blocks * SLOTS, (p + 1) * blocks * SLOTS)
        dg = (tall[rows, :] * gate_f[rows, :]).astype(BF)
        du = (tall[rows, :] * up_f[rows, :]).astype(BF)
        d_gate[rows, :] = dg
        d_up[rows, :] = du
        for c in range(CORES):
            cols = slice(c * half, (c + 1) * half)
            piece = (dot(dg, gate_v[:, cols]) + dot(du, up_v[:, cols])).astype(BF)
            y[c, span] = piece.reshape(blocks, SLOTS, half)
            i = CORES * p + c
            store = pltpu.make_async_copy(y.at[c, span], out.at[span, c], out_sem.at[i])
            store.start()
            stores.append(store)
    for store in stores:
        store.wait()


def grads_kernel(
    where, rows_in, d_mixed, place, hidden, d_gate, d_up, g_gate, g_up, g_down, spread
):
    block = 64
    half = d_mixed.shape[3]
    for b in range(d_mixed.shape[0]):
        rows = slice(b * SLOTS, (b + 1) * SLOTS)
        part = dot(place[rows, :], hidden[rows, :], 0, 0)
        spread[b * block : (b + 1) * block, :] = part.astype(BF)
    for c in range(CORES):
        part = d_mixed[:, c].reshape(spread.shape[0], half)
        g_down[:, c * half : (c + 1) * half] = dot(spread[...], part, 0, 0).astype(BF)
    g_gate[...] = dot(d_gate[...], rows_in[...], 0, 0).astype(BF)
    g_up[...] = dot(d_up[...], rows_in[...], 0, 0).astype(BF)


def combine_kernel(where, returned, ids, weight, d_mixed, mixed, route, place):
    first_expert, core = where[0], where[1]
    rows = ids.shape[0]
    count, half = returned.shape
    lane = iota((rows, count), 1)
    source = lane // SLOTS
    sources_per_expert = count // SLOTS // EXP_DEV
    expert = first_expert + (source % CORES) * EXP_DEV + source // sources_per_expert
    all_ids = ids[...]
    pick = rows_of_slots(all_ids, expert, lane % SLOTS)
    place[...] = pick.astype(BF)
    scale = jnp.zeros((rows, count), F32)
    for k in range(ids.shape[1]):
        scale = scale + jnp.where(all_ids[:, k : k + 1] == expert, weight[:, k : k + 1], 0.0)
    high, low = split(pick * scale)
    back = returned[...]
    mixed[...] = dot(high, back) + dot(low, back)
    own_grad = d_mixed[:, pl.ds(pl.multiple_of(core * half, LANES), half)]
    paired = dot(own_grad, back, 1, 1) * pick
    spot = iota((rows, LANES), 1)
    result = jnp.zeros((rows, LANES), F32)
    for k in range(ids.shape[1]):
        mine = jnp.where(all_ids[:, k : k + 1] == expert, paired, 0.0)
        result = jnp.where(spot % 8 == k, jnp.sum(mine, axis=1, keepdims=True), result)
    route[...] = result


def pack_kernel(where, returned, place, mixed, route, out, back, in_sem):
    half = returned.shape[1]
    step = back.shape[0] // in_sem.shape[0]
    spans = [slice(i * step, (i + 1) * step) for i in range(in_sem.shape[0])]
    loads = begin([(returned.at[span], back.at[span]) for span in spans], in_sem)
    high, low = split(route[...])
    for i in range(out.shape[0] // 2):
        rows = slice(8 * i, 8 * i + 8)
        out[2 * i, :, :half] = mixed[rows, :].astype(BF)
        out[2 * i, :, half:] = high.astype(F32)[rows].astype(BF)
        out[2 * i + 1, :, half:] = low.astype(F32)[rows].astype(BF)
    total = jnp.zeros((place.shape[0], half), F32)
    for span, load in zip(spans, loads):
        load.wait()
        total = total + dot(place[:, span], back[span])
    for i in range(out.shape[0] // 2):
        out[2 * i + 1, :, :half] = total[8 * i : 8 * i + 8].astype(BF)


def total_kernel(where, parts, out):
    total = parts[0].astype(F32)
    for i in range(1, parts.shape[0]):
        total = total + parts[i].astype(F32)
    width = total.shape[1] - LANES
    tail = total[:, width:]
    high, low = split(tail)
    spot = iota(tail.shape, 1)
    tail = jnp.where(spot < 8, high.astype(F32), low.astype(F32)).astype(BF)
    body_part = total[:, :width].astype(BF)
    for i in range(out.shape[0]):
        out[i, :, :width] = body_part
        out[i, :, width:] = tail


def finish_kernel(where, own, other, mixed, d_tokens, route):
    core = where[0]
    width = own.shape[2] - LANES
    for source, side in ((own, core), (other, 1 - core)):
        cols = pl.ds(pl.multiple_of(side * width, LANES), width)
        for target, odd in ((mixed, 0), (d_tokens, 1)):
            for i in range(0, own.shape[0] // 2, 2):
                pair = [source[2 * (i + j) + odd, :, :width].astype(F32) for j in range(2)]
                target[8 * i : 8 * i + 16, cols] = jnp.concatenate(pair, axis=0).astype(BF)
    parts = []
    for i in range(own.shape[0] // 2):
        total = jnp.zeros((8, LANES), F32)
        for source in (own, other):
            for odd in range(2):
                total = total + source[2 * i + odd, :, width:].astype(F32)
        parts.append(total)
    total = jnp.concatenate(parts, axis=0).T
    count = route.shape[0]
    route[...] = total[:count] + total[8 : 8 + count]


def body(tokens, d_mixed, route_ids, route_weight, gate_weight, up_weight, down_weight):
    dp_count = lax.axis_size("dp")
    z_count = lax.axis_size("z")
    dp_index, z_index, core = lax.axis_index("dp"), lax.axis_index("z"), lax.axis_index("core")
    row_count, width = tokens.shape
    half = width // CORES
    hidden_count = gate_weight.shape[1]
    total = dp_count * row_count
    slot_rows = dp_count * SLOTS
    dma = pltpu.SemaphoreType.DMA
    chip_expert = z_index * CORES * EXP_DEV
    column_expert = chip_expert + core * EXP_DEV
    expert = column_expert + dp_index // (dp_count // EXP_DEV)
    gate_piece, up_piece, down_piece = gate_weight[0], up_weight[0], down_weight[0]
    weight_v = pltpu.VMEM((hidden_count, width), BF)
    sent_shape = (dp_count, CORES, SLOTS, half)

    own_half = lax.dynamic_slice_in_dim(d_mixed, core * half, half, 1)
    all_grad = lax.all_gather(own_half, ("dp", "core"), axis=0, tiled=True)
    all_grad = all_grad.reshape(dp_count, CORES, row_count, half)

    own_ids = lax.dynamic_slice_in_dim(route_ids, dp_index * row_count, row_count, 0)
    (sent,) = call(
        send_kernel,
        [((dp_count, SLOTS, width), BF, ANY)],
        [column_expert],
        [(own_ids.T, VMEM), (tokens, ANY)],
        [
            pltpu.VMEM((row_count, width), BF),
            pltpu.VMEM((EXP_DEV, SLOTS, width), BF),
            dma((1,)),
            dma((dp_count,)),
        ],
    )
    route_ids, route_weight, own_ids, sent = lax.optimization_barrier(
        (route_ids, route_weight, own_ids, sent)
    )
    own_weight = lax.dynamic_slice_in_dim(route_weight, dp_index * row_count, row_count, 0)
    rows_in = lax.all_to_all(sent, "dp", 0, 0, tiled=True)

    (out,) = call(
        forward_kernel,
        [(sent_shape, BF, ANY)],
        [expert],
        [(rows_in, ANY), (gate_piece, ANY), (up_piece, ANY), (down_piece, ANY)],
        [
            pltpu.VMEM((dp_count, SLOTS, width), BF),
            weight_v,
            weight_v,
            weight_v,
            pltpu.VMEM((CORES, dp_count, SLOTS, half), BF),
            dma((5,)),
            dma((4,)),
        ],
    )
    out, rows_in = lax.optimization_barrier((out, rows_in))
    rows_in = rows_in.reshape(slot_rows, width)
    returned = lax.all_to_all(
        out.reshape(CORES * dp_count, SLOTS, half), ("dp", "core"), 0, 0, tiled=True
    )
    place, gate_factor, up_factor, hidden = call(
        factors_kernel,
        [
            ((slot_rows, row_count), BF, VMEM),
            ((slot_rows, hidden_count), F32, VMEM),
            ((slot_rows, hidden_count), F32, VMEM),
            ((slot_rows, hidden_count), BF, VMEM),
        ],
        [expert],
        [
            (rows_in, VMEM),
            (gate_piece, VMEM),
            (up_piece, VMEM),
            (route_ids.T, VMEM),
            (route_weight.T, VMEM),
        ],
    )

    out_in, d_gate, d_up = call(
        backward_kernel,
        [
            (sent_shape, BF, ANY),
            ((slot_rows, hidden_count), BF, VMEM),
            ((slot_rows, hidden_count), BF, VMEM),
        ],
        [expert],
        [
            (all_grad, ANY),
            (place, ANY),
            (gate_factor, ANY),
            (up_factor, ANY),
            (gate_piece, ANY),
            (up_piece, ANY),
            (down_piece, ANY),
        ],
        [
            pltpu.VMEM((dp_count, CORES, row_count, half), BF),
            pltpu.VMEM((slot_rows, row_count), BF),
            pltpu.VMEM((slot_rows, hidden_count), F32),
            pltpu.VMEM((slot_rows, hidden_count), F32),
            weight_v,
            weight_v,
            weight_v,
            pltpu.VMEM((slot_rows, hidden_count), F32),
            pltpu.VMEM((CORES, dp_count, SLOTS, half), BF),
            dma((8,)),
            dma((4,)),
        ],
    )
    out_in, d_gate, returned = lax.optimization_barrier((out_in, d_gate, returned))
    returned_in = lax.all_to_all(
        out_in.reshape(CORES * dp_count, SLOTS, half), ("dp", "core"), 0, 0, tiled=True
    )
    grads = call(
        grads_kernel,
        [((hidden_count, width), BF, VMEM)] * 3,
        [expert],
        [
            (rows_in, VMEM),
            (all_grad, VMEM),
            (place, VMEM),
            (hidden, VMEM),
            (d_gate, VMEM),
            (d_up, VMEM),
        ],
        [pltpu.VMEM((total, hidden_count), BF)],
    )
    mixed_part, route_part, own_place = call(
        combine_kernel,
        [
            ((row_count, half), F32, VMEM),
            ((row_count, LANES), F32, VMEM),
            ((row_count, CORES * slot_rows), BF, VMEM),
        ],
        [chip_expert, core],
        [
            (returned.reshape(CORES * slot_rows, half), VMEM),
            (own_ids, VMEM),
            (own_weight, VMEM),
            (d_mixed, VMEM),
        ],
    )
    grad_gate, grad_up, grad_down, own_place = lax.optimization_barrier((*grads, own_place))
    (packed,) = call(
        pack_kernel,
        [((z_count, 8, half + LANES), BF, VMEM)],
        [core],
        [
            (returned_in.reshape(CORES * slot_rows, half), ANY),
            (own_place, VMEM),
            (mixed_part, VMEM),
            (route_part, VMEM),
        ],
        [pltpu.VMEM((CORES * slot_rows, half), BF), dma((4,))],
    )
    parts = lax.all_to_all(packed, "z", 0, 0, tiled=True)
    (summed,) = call(
        total_kernel, [((z_count, 8, half + LANES), BF, VMEM)], [core], [(parts, VMEM)]
    )
    whole = lax.all_to_all(summed, "z", 0, 0, tiled=True)
    other = lax.ppermute(whole, "core", [(0, 1), (1, 0)])
    mixed, d_tokens, d_route = call(
        finish_kernel,
        [
            ((row_count, width), BF, VMEM),
            ((row_count, width), BF, VMEM),
            ((route_ids.shape[1], row_count), F32, VMEM),
        ],
        [core],
        [(whole, VMEM), (other, VMEM)],
    )
    return (mixed, d_route.T, d_tokens, grad_gate[None], grad_up[None], grad_down[None])


def solution(mesh):
    dp_count, expert_count = mesh.devices.shape
    fine = Mesh(
        mesh.devices.reshape(dp_count, expert_count // CORES, CORES), ("dp", "z", "core")
    )
    rows = P("dp", None)
    blocks = P(("z", "core", "dp"), None, None)
    in_specs = (rows, rows, P(), P(), blocks, blocks, blocks)
    out_specs = (rows, rows, rows, blocks, blocks, blocks)
    return jax.shard_map(body, mesh=fine, in_specs=in_specs, out_specs=out_specs, check_vma=False)
```

```python
import math

import jax
import jax.numpy as jnp
from jax import lax
from jax.experimental import pallas as pl
from jax.experimental.pallas import tpu as pltpu
from jax.sharding import Mesh, PartitionSpec as P

CORES = 2
EXP_DEV = 2
SLOTS = 30
ROWS = 32
LANES = 128
BF = jnp.bfloat16
F32 = jnp.float32


def dot(left, right, left_dim=1, right_dim=0):
    return lax.dot_general(
        left, right, (((left_dim,), (right_dim,)), ((), ())), preferred_element_type=F32
    )


def iota(shape, dim):
    return lax.broadcasted_iota(jnp.int32, shape, dim)


def split(value):
    high = value.astype(BF)
    return high, (value - high.astype(F32)).astype(BF)


def slot_rows_of(ids, expert, slot):
    count = ids.shape[1]
    hit = ids[0:1, :] == expert
    for k in range(1, ids.shape[0]):
        hit = jnp.logical_or(hit, ids[k : k + 1, :] == expert)
    flag = hit.astype(F32)
    earlier = (iota((count, count), 0) < iota((count, count), 1)).astype(BF)
    return jnp.where(dot(flag.astype(BF), earlier) == slot.astype(F32), flag, 0.0)


def rows_of_slots(ids, expert, slot):
    count = ids.shape[0]
    hit = ids[:, 0:1] == expert
    for k in range(1, ids.shape[1]):
        hit = jnp.logical_or(hit, ids[:, k : k + 1] == expert)
    flag = hit.astype(F32)
    earlier = (iota((count, count), 1) < iota((count, count), 0)).astype(BF)
    return jnp.where(dot(earlier, flag.astype(BF)) == slot.astype(F32), flag, 0.0)


VMEM = pl.BlockSpec(memory_space=pltpu.VMEM)
HBM = pl.BlockSpec(memory_space=pltpu.HBM)


def call(kernel, outs, scalars, arrays, scratch=(), vmem=8):
    ins = [i for i, (_, space) in enumerate(arrays) if space is HBM]
    kept = [i for i, (_, _, space) in enumerate(outs) if space is HBM]
    count, total = len(arrays), len(arrays) + len(outs)

    def wrapped(where, *refs):
        given, results, rest = list(refs[:count]), list(refs[count:total]), list(refs[total:])
        in_sem, out_sem = rest.pop(), rest.pop()
        loads = {}
        for n, i in enumerate(ins):
            loads[i] = pltpu.make_async_copy(given[i], rest[n], in_sem.at[n])
            loads[i].start()
            given[i] = rest[n]
        rest = rest[len(ins) :]
        targets = {}
        for n, i in enumerate(kept):
            targets[i] = (results[i], out_sem.at[n])
            results[i] = rest[n]
        rest = rest[len(kept) :]
        stores = []

        def ready(*names):
            for i in names:
                if i in loads:
                    loads.pop(i).wait()

        def done(i):
            target, sem = targets.pop(i)
            stores.append(pltpu.make_async_copy(results[i], target, sem))
            stores[-1].start()

        kernel(where, ready, done, *given, *results, *rest)
        ready(*list(loads))
        for i in list(targets):
            done(i)
        for store in stores:
            store.wait()

    def held(array, space):
        return pltpu.with_memory_space_constraint(array, pltpu.HBM) if space is HBM else array

    def result(shape, kind, space):
        return pltpu.HBM(shape, kind) if space is HBM else jax.ShapeDtypeStruct(shape, kind)

    dma = pltpu.SemaphoreType.DMA
    return pl.pallas_call(
        wrapped,
        out_shape=[result(*out) for out in outs],
        in_specs=[pl.BlockSpec(memory_space=pltpu.SMEM)] + [space for _, space in arrays],
        out_specs=[space for _, _, space in outs],
        scratch_shapes=[pltpu.VMEM(arrays[i][0].shape, arrays[i][0].dtype) for i in ins]
        + [pltpu.VMEM(outs[i][0], outs[i][1]) for i in kept]
        + list(scratch)
        + [dma((max(1, len(kept)),)), dma((max(1, len(ins)),))],
        compiler_params=pltpu.CompilerParams(vmem_limit_bytes=vmem << 20),
    )(jnp.stack(scalars).astype(jnp.int32), *[held(*array) for array in arrays])


def padded(block):
    extra = jnp.zeros((ROWS - block.shape[0], block.shape[1]), F32)
    return jnp.concatenate([block.astype(F32), extra], axis=0)


def send_kernel(where, ready, done, ids, tokens, out):
    spot = iota((EXP_DEV * ROWS, 1), 0)
    pick = slot_rows_of(ids[...], where[0] + spot // ROWS, spot % ROWS).astype(BF)
    ready(1)
    picked = dot(pick, tokens[...]).astype(BF)
    per_expert = out.shape[0] // EXP_DEV
    for d in range(out.shape[0]):
        first = d // per_expert * ROWS
        out[d] = picked[first : first + SLOTS]


def weights_of_slots(expert, ids, weight):
    slot = iota((ROWS, 1), 0)
    pick = slot_rows_of(ids, jnp.full((ROWS, 1), expert, jnp.int32), slot)
    scale = jnp.zeros((1, ids.shape[1]), F32)
    for k in range(ids.shape[0]):
        scale = scale + jnp.where(ids[k : k + 1, :] == expert, weight[k : k + 1, :], 0.0)
    return jnp.sum(pick * scale, axis=1, keepdims=True)


def forward_kernel(
    where, ready, done, ids, weight, rows_in, gate_w, up_w, down_w,
    out, x, gate_factor, up_factor, hidden
):
    blocks = rows_in.shape[0]
    block = ids.shape[1] // blocks
    half = out.shape[2]
    for b in range(blocks):
        x[b * ROWS : (b + 1) * ROWS, :] = padded(rows_in[b]).astype(BF)
    done(1)
    ready(3, 4)
    g = dot(x[...], gate_w[...], 1, 1)
    u = dot(x[...], up_w[...], 1, 1)
    sig = jax.nn.sigmoid(g)
    act = g * sig
    h = (act * u).astype(BF)
    ready(5)
    for c in range(CORES):
        piece = dot(h, down_w[:, c * half : (c + 1) * half]).astype(BF)
        for d in range(blocks):
            out[CORES * d + c] = piece[d * ROWS : d * ROWS + SLOTS]
    done(0)
    gate_factor[...] = u * sig * (1.0 + g * (1.0 - sig))
    up_factor[...] = act
    hidden[...] = h
    for b in range(blocks):
        cols, rows = slice(b * block, (b + 1) * block), slice(b * ROWS, (b + 1) * ROWS)
        scale = weights_of_slots(where[0], ids[:, cols], weight[:, cols])
        gate_factor[rows, :] = gate_factor[rows, :] * scale
        up_factor[rows, :] = up_factor[rows, :] * scale
        hidden[rows, :] = (hidden[rows, :].astype(F32) * scale).astype(BF)


def backward_kernel(
    where, ready, done, rows_grad, down_w, gate_factor, up_factor, gate_w, up_w,
    out, rows, d_gate, d_up
):
    blocks = rows_grad.shape[0]
    half = out.shape[2]
    ready(0)
    for b in range(blocks):
        rows[b * ROWS : (b + 1) * ROWS, :] = padded(rows_grad[b]).astype(BF)
    ready(1)
    d_hidden = dot(rows[...], down_w[...], 1, 1)
    ready(2, 3)
    dg = (d_hidden * gate_factor[...]).astype(BF)
    du = (d_hidden * up_factor[...]).astype(BF)
    ready(4, 5)
    for c in range(CORES):
        cols = slice(c * half, (c + 1) * half)
        piece = (dot(dg, gate_w[:, cols]) + dot(du, up_w[:, cols])).astype(BF)
        for d in range(blocks):
            out[CORES * d + c] = piece[d * ROWS : d * ROWS + SLOTS]
    done(0)
    d_gate[...] = dg
    d_up[...] = du


def grads_kernel(
    where, ready, done, x, rows_grad, hidden, d_gate, d_up, g_gate, g_up, g_down
):
    ready(1, 2)
    g_down[...] = dot(hidden[...], rows_grad[...], 0, 0).astype(BF)
    done(2)
    ready(0, 3)
    g_gate[...] = dot(d_gate[...], x[...], 0, 0).astype(BF)
    done(0)
    ready(4)
    g_up[...] = dot(d_up[...], x[...], 0, 0).astype(BF)


def gathered(returned, total):
    sources = returned.shape[0]
    pieces = sources // CORES // EXP_DEV
    for j in range(EXP_DEV):
        for c in range(CORES):
            part = None
            for d in range(j * pieces, (j + 1) * pieces):
                block = returned[CORES * d + c].astype(F32)
                part = block if part is None else part + block
            first = (CORES * j + c) * ROWS
            total[first : first + ROWS, :] = padded(part)
    return split(total[...])


def combine_kernel(
    where, ready, done, returned, ids, weight, d_mixed, mixed, route, place, total
):
    first_expert, core = where[0], where[1]
    rows = ids.shape[0]
    half = returned.shape[2]
    count = total.shape[0]
    lane = iota((rows, count), 1)
    source = lane // ROWS
    expert = first_expert + (source % CORES) * EXP_DEV + source // CORES
    all_ids = ids[...]
    pick = rows_of_slots(all_ids, expert, lane % ROWS)
    place[...] = pick.astype(BF)
    scale = jnp.zeros((rows, count), F32)
    for k in range(ids.shape[1]):
        scale = scale + jnp.where(all_ids[:, k : k + 1] == expert, weight[:, k : k + 1], 0.0)
    high, low = split(pick * scale)
    ready(0)
    back, rest = gathered(returned, total)
    mixed[...] = dot(high, back) + (dot(low, back) + dot(high, rest))
    ready(3)
    own_grad = d_mixed[:, pl.ds(pl.multiple_of(core * half, LANES), half)]
    paired = (dot(own_grad, back, 1, 1) + dot(own_grad, rest, 1, 1)) * pick
    spot = iota((rows, LANES), 1)
    result = jnp.zeros((rows, LANES), F32)
    for k in range(ids.shape[1]):
        mine = jnp.where(all_ids[:, k : k + 1] == expert, paired, 0.0)
        result = jnp.where(spot % 8 == k, jnp.sum(mine, axis=1, keepdims=True), result)
    route[...] = result


def pack_kernel(where, ready, done, returned, place, mixed, route, out, total):
    half = returned.shape[2]
    high, low = split(route[...])
    for i in range(out.shape[0] // 2):
        rows = slice(8 * i, 8 * i + 8)
        out[2 * i, :, :half] = mixed[rows, :].astype(BF)
        out[2 * i, :, half:] = high.astype(F32)[rows].astype(BF)
        out[2 * i + 1, :, half:] = low.astype(F32)[rows].astype(BF)
    ready(0)
    back, rest = gathered(returned, total)
    sums = dot(place[...], back) + dot(place[...], rest)
    for i in range(out.shape[0] // 2):
        out[2 * i + 1, :, :half] = sums[8 * i : 8 * i + 8].astype(BF)


def total_kernel(where, ready, done, parts, out):
    total = parts[0].astype(F32)
    for i in range(1, parts.shape[0]):
        total = total + parts[i].astype(F32)
    width = total.shape[1] - LANES
    tail = total[:, width:]
    high, low = split(tail)
    spot = iota(tail.shape, 1)
    tail = jnp.where(spot < 8, high.astype(F32), low.astype(F32)).astype(BF)
    body_part = total[:, :width].astype(BF)
    for i in range(out.shape[0]):
        out[i, :, :width] = body_part
        out[i, :, width:] = tail


def finish_kernel(where, ready, done, own, other, mixed, d_tokens, route):
    core = where[0]
    width = own.shape[2] - LANES
    for source, side in ((own, core), (other, 1 - core)):
        cols = pl.ds(pl.multiple_of(side * width, LANES), width)
        for target, odd in ((mixed, 0), (d_tokens, 1)):
            for i in range(0, own.shape[0] // 2, 2):
                pair = [source[2 * (i + j) + odd, :, :width].astype(F32) for j in range(2)]
                target[8 * i : 8 * i + 16, cols] = jnp.concatenate(pair, axis=0).astype(BF)
    parts = []
    for i in range(own.shape[0] // 2):
        total = jnp.zeros((8, LANES), F32)
        for source in (own, other):
            for odd in range(2):
                total = total + source[2 * i + odd, :, width:].astype(F32)
        parts.append(total)
    total = jnp.concatenate(parts, axis=0).T
    count = route.shape[0]
    route[...] = total[:count] + total[8 : 8 + count]


def body(tokens, d_mixed, route_ids, route_weight, gate_weight, up_weight, down_weight):
    side = lax.axis_size("y")
    dp_count = lax.axis_size("x") * side
    z_count = lax.axis_size("z")
    z_index, core = lax.axis_index("z"), lax.axis_index("core")
    dp_index = lax.axis_index("x") * side + lax.axis_index("y")
    row_count, width = tokens.shape
    half = width // CORES
    hidden_count = gate_weight.shape[1]
    rows = dp_count * ROWS
    chip_expert = z_index * CORES * EXP_DEV
    column_expert = chip_expert + core * EXP_DEV
    expert = column_expert + dp_index // (dp_count // EXP_DEV)
    gate_piece, up_piece, down_piece = gate_weight[0], up_weight[0], down_weight[0]
    out_shape = (CORES * dp_count, SLOTS, half)
    gathered_v = pltpu.VMEM((CORES * EXP_DEV * ROWS, half), F32)

    def own_rows(array):
        return lax.dynamic_slice_in_dim(array, dp_index * row_count, row_count, 0)

    def send(array, ids):
        (sent,) = call(
            send_kernel,
            [((dp_count, SLOTS, width), BF, HBM)],
            [column_expert],
            [(ids, VMEM), (array, HBM)],
        )
        return sent

    sent = send(tokens, own_rows(route_ids).T)
    sent, route_ids, route_weight = lax.optimization_barrier((sent, route_ids, route_weight))
    rows_in = lax.all_to_all(sent, ("x", "y"), 0, 0, tiled=True)
    sent_grad = send(d_mixed, own_rows(route_ids).T)
    rows_grad = lax.all_to_all(sent_grad, ("x", "y"), 0, 0, tiled=True)

    out, x, gate_factor, up_factor, hidden = call(
        forward_kernel,
        [
            (out_shape, BF, HBM),
            ((rows, width), BF, HBM),
            ((rows, hidden_count), F32, HBM),
            ((rows, hidden_count), F32, HBM),
            ((rows, hidden_count), BF, HBM),
        ],
        [expert],
        [
            (route_ids.T, VMEM),
            (route_weight.T, VMEM),
            (rows_in, VMEM),
            (gate_piece, HBM),
            (up_piece, HBM),
            (down_piece, HBM),
        ],
        vmem=24,
    )
    out, rows_grad = lax.optimization_barrier((out, rows_grad))
    returned = lax.all_to_all(out, ("x", "y", "core"), 0, 0, tiled=True)

    out_in, padded_grad, d_gate, d_up = call(
        backward_kernel,
        [
            (out_shape, BF, HBM),
            ((rows, width), BF, HBM),
            ((rows, hidden_count), BF, HBM),
            ((rows, hidden_count), BF, HBM),
        ],
        [expert],
        [
            (rows_grad, HBM),
            (down_piece, HBM),
            (gate_factor, HBM),
            (up_factor, HBM),
            (gate_piece, HBM),
            (up_piece, HBM),
        ],
        vmem=24,
    )
    grads = call(
        grads_kernel,
        [((hidden_count, width), BF, HBM)] * 3,
        [expert],
        [(x, HBM), (padded_grad, HBM), (hidden, HBM), (d_gate, HBM), (d_up, HBM)],
        vmem=24,
    )
    grad_gate, grad_up, grad_down, out_in, route_ids, route_weight = lax.optimization_barrier(
        (*grads, out_in, route_ids, route_weight)
    )
    returned_in = lax.all_to_all(out_in, ("x", "y", "core"), 0, 0, tiled=True)
    mixed_part, route_part, own_place = call(
        combine_kernel,
        [
            ((row_count, half), F32, VMEM),
            ((row_count, LANES), F32, VMEM),
            ((row_count, CORES * EXP_DEV * ROWS), BF, VMEM),
        ],
        [chip_expert, core],
        [
            (returned, VMEM),
            (own_rows(route_ids), VMEM),
            (own_rows(route_weight), VMEM),
            (d_mixed, HBM),
        ],
        [gathered_v],
        vmem=16,
    )
    (packed,) = call(
        pack_kernel,
        [((z_count, 8, half + LANES), BF, VMEM)],
        [core],
        [(returned_in, VMEM), (own_place, VMEM), (mixed_part, VMEM), (route_part, VMEM)],
        [gathered_v],
    )
    parts = lax.all_to_all(packed, "z", 0, 0, tiled=True)
    (summed,) = call(
        total_kernel, [((z_count, 8, half + LANES), BF, VMEM)], [core], [(parts, VMEM)]
    )
    whole = lax.all_to_all(summed, "z", 0, 0, tiled=True)
    other = lax.ppermute(whole, "core", [(0, 1), (1, 0)])
    mixed, d_tokens, d_route = call(
        finish_kernel,
        [
            ((row_count, width), BF, VMEM),
            ((row_count, width), BF, VMEM),
            ((route_ids.shape[1], row_count), F32, VMEM),
        ],
        [core],
        [(whole, VMEM), (other, VMEM)],
    )
    return (mixed, d_route.T, d_tokens, grad_gate[None], grad_up[None], grad_down[None])


def solution(mesh):
    dp_count, expert_count = mesh.devices.shape
    side = math.isqrt(dp_count)
    fine = Mesh(
        mesh.devices.reshape(side, side, expert_count // CORES, CORES), ("x", "y", "z", "core")
    )
    rows = P(("x", "y"), None)
    blocks = P(("z", "core", "x", "y"), None, None)
    in_specs = (rows, rows, P(), P(), blocks, blocks, blocks)
    out_specs = (rows, rows, rows, blocks, blocks, blocks)
    return jax.shard_map(body, mesh=fine, in_specs=in_specs, out_specs=out_specs, check_vma=False)
```

```python
import math

import jax
import jax.numpy as jnp
from jax import lax
from jax.experimental import pallas as pl
from jax.experimental.pallas import tpu as pltpu
from jax.sharding import Mesh, PartitionSpec as P

CORES = 2
EXP_DEV = 2
SLOTS = 30
ROWS = 32
LANES = 128
BF = jnp.bfloat16
F32 = jnp.float32


def dot(left, right, left_dim=1, right_dim=0):
    return lax.dot_general(
        left, right, (((left_dim,), (right_dim,)), ((), ())), preferred_element_type=F32
    )


def iota(shape, dim):
    return lax.broadcasted_iota(jnp.int32, shape, dim)


def split(value):
    high = value.astype(BF)
    return high, (value - high.astype(F32)).astype(BF)


def slot_rows_of(ids, expert, slot, block):
    count = ids.shape[1]
    hit = ids[0:1, :] == expert
    for k in range(1, ids.shape[0]):
        hit = jnp.logical_or(hit, ids[k : k + 1, :] == expert)
    flag = hit.astype(F32)
    before, after = iota((count, count), 0), iota((count, count), 1)
    earlier = jnp.logical_and(before < after, before // block == after // block).astype(BF)
    return jnp.where(dot(flag.astype(BF), earlier) == slot.astype(F32), flag, 0.0)


def rows_of_slots(ids, expert, slot):
    count = ids.shape[0]
    hit = ids[:, 0:1] == expert
    for k in range(1, ids.shape[1]):
        hit = jnp.logical_or(hit, ids[:, k : k + 1] == expert)
    flag = hit.astype(F32)
    earlier = (iota((count, count), 1) < iota((count, count), 0)).astype(BF)
    return jnp.where(dot(earlier, flag.astype(BF)) == slot.astype(F32), flag, 0.0)


VMEM = pl.BlockSpec(memory_space=pltpu.VMEM)
HBM = pl.BlockSpec(memory_space=pltpu.HBM)


def begin(pairs, sems):
    copies = [pltpu.make_async_copy(a, b, sems.at[i]) for i, (a, b) in enumerate(pairs)]
    for copy in copies:
        copy.start()
    return copies


def call(kernel, outs, scalars, arrays, scratch=(), vmem=8):
    ins = [i for i, (_, space) in enumerate(arrays) if space is HBM]
    kept = [i for i, (_, _, space) in enumerate(outs) if space is HBM]
    count, total = len(arrays), len(arrays) + len(outs)

    def wrapped(where, *refs):
        given, results, rest = list(refs[:count]), list(refs[count:total]), list(refs[total:])
        in_sem, out_sem = rest.pop(), rest.pop()
        loads = {}
        for n, i in enumerate(ins):
            loads[i] = pltpu.make_async_copy(given[i], rest[n], in_sem.at[n])
            loads[i].start()
            given[i] = rest[n]
        rest = rest[len(ins) :]
        targets = {}
        for n, i in enumerate(kept):
            targets[i] = (results[i], out_sem.at[n])
            results[i] = rest[n]
        rest = rest[len(kept) :]
        stores = []

        def ready(*names):
            for i in names:
                if i in loads:
                    loads.pop(i).wait()

        def done(i):
            target, sem = targets.pop(i)
            stores.append(pltpu.make_async_copy(results[i], target, sem))
            stores[-1].start()

        kernel(where, ready, done, *given, *results, *rest)
        ready(*list(loads))
        for i in list(targets):
            done(i)
        for store in stores:
            store.wait()

    def held(array, space):
        return pltpu.with_memory_space_constraint(array, pltpu.HBM) if space is HBM else array

    def result(shape, kind, space):
        return pltpu.HBM(shape, kind) if space is HBM else jax.ShapeDtypeStruct(shape, kind)

    dma = pltpu.SemaphoreType.DMA
    return pl.pallas_call(
        wrapped,
        out_shape=[result(*out) for out in outs],
        in_specs=[pl.BlockSpec(memory_space=pltpu.SMEM)] + [space for _, space in arrays],
        out_specs=[space for _, _, space in outs],
        scratch_shapes=[pltpu.VMEM(arrays[i][0].shape, arrays[i][0].dtype) for i in ins]
        + [pltpu.VMEM(outs[i][0], outs[i][1]) for i in kept]
        + list(scratch)
        + [dma((max(1, len(kept)),)), dma((max(1, len(ins)),))],
        compiler_params=pltpu.CompilerParams(vmem_limit_bytes=vmem << 20),
    )(jnp.stack(scalars).astype(jnp.int32), *[held(*array) for array in arrays])


def padded(block):
    extra = jnp.zeros((ROWS - block.shape[0], block.shape[1]), F32)
    return jnp.concatenate([block.astype(F32), extra], axis=0)


def send_kernel(where, ready, done, ids, tokens, out):
    spot = iota((EXP_DEV * ROWS, 1), 0)
    pick = slot_rows_of(ids[...], where[0] + spot // ROWS, spot % ROWS, ids.shape[1]).astype(BF)
    ready(1)
    picked = dot(pick, tokens[...]).astype(BF)
    per_expert = out.shape[0] // EXP_DEV
    for d in range(out.shape[0]):
        first = d // per_expert * ROWS
        out[d] = picked[first : first + SLOTS]


def weights_of_slots(expert, ids, weight, block):
    slot = iota((ROWS, 1), 0)
    pick = slot_rows_of(ids, jnp.full((ROWS, 1), expert, jnp.int32), slot, block)
    scale = jnp.zeros((1, ids.shape[1]), F32)
    for k in range(ids.shape[0]):
        scale = scale + jnp.where(ids[k : k + 1, :] == expert, weight[k : k + 1, :], 0.0)
    scale = pick * scale
    owner = iota(scale.shape, 1) // block
    return [
        jnp.sum(jnp.where(owner == j, scale, 0.0), axis=1, keepdims=True)
        for j in range(ids.shape[1] // block)
    ]


def prepare_kernel(where, ids, rows, all_ids, all_weight, *refs):
    out, scale, rows_v, ids_v, weight_v, picked, scale_v = refs[-7:]

    @pl.when(where[1] == where[2])
    def _():
        pltpu.sync_copy(rows, rows_v)
        send_kernel(where, lambda _: None, None, ids, rows_v, picked)
        pltpu.sync_copy(picked, out)
        pltpu.sync_copy(all_ids, ids_v)
        pltpu.sync_copy(all_weight, weight_v)
        block = ids.shape[1]
        per_step = LANES // block

        def some_blocks(i, carry):
            cols = pl.ds(pl.multiple_of(i * LANES, LANES), LANES)
            parts = weights_of_slots(where[3], ids_v[:, cols], weight_v[:, cols], block)
            for j, part in enumerate(parts):
                first = pl.multiple_of((i * per_step + j) * ROWS, ROWS)
                scale_v[pl.ds(first, ROWS), :] = part
            return carry

        lax.fori_loop(0, all_ids.shape[1] // LANES, some_blocks, 0)
        pltpu.sync_copy(scale_v, scale)


def prepare(turn, core, experts, ids, rows, all_ids, all_weight, shapes, before=()):
    arrays = [
        pltpu.with_memory_space_constraint(array, pltpu.HBM)
        for array in (rows, all_ids, all_weight, *before)
    ]
    (out, out_kind), (scale, scale_kind) = shapes
    return pl.pallas_call(
        prepare_kernel,
        out_shape=[pltpu.HBM(out, out_kind), pltpu.HBM(scale, scale_kind)],
        in_specs=[pl.BlockSpec(memory_space=pltpu.SMEM), VMEM] + [HBM] * len(arrays),
        out_specs=[HBM, HBM],
        input_output_aliases={5: 0, 6: 1} if before else {},
        scratch_shapes=[
            pltpu.VMEM(rows.shape, rows.dtype),
            pltpu.VMEM(all_ids.shape, all_ids.dtype),
            pltpu.VMEM(all_weight.shape, all_weight.dtype),
            pltpu.VMEM(out, out_kind),
            pltpu.VMEM(scale, scale_kind),
        ],
        compiler_params=pltpu.CompilerParams(vmem_limit_bytes=8 << 20),
    )(jnp.stack([experts[0], core, jnp.int32(turn), experts[1]]).astype(jnp.int32), ids, *arrays)


def forward_kernel(
    where, ready, done, scale, rows_in, gate_w, up_w, down_w,
    out, x, gate_factor, up_factor, hidden
):
    blocks = rows_in.shape[0]
    half = out.shape[2] // CORES
    for b in range(blocks):
        x[b * ROWS : (b + 1) * ROWS, :] = padded(rows_in[b]).astype(BF)
    done(1)
    ready(2, 3)
    g = dot(x[...], gate_w[...], 1, 1)
    u = dot(x[...], up_w[...], 1, 1)
    sig = jax.nn.sigmoid(g)
    act = g * sig
    h = (act * u).astype(BF)
    ready(4)
    for c in range(CORES):
        cols = slice(c * half, (c + 1) * half)
        piece = dot(h, down_w[:, cols]).astype(BF)
        for d in range(blocks):
            out[d, :, cols] = piece[d * ROWS : d * ROWS + SLOTS]
    done(0)
    ready(0)
    gate_factor[...] = u * sig * (1.0 + g * (1.0 - sig)) * scale[...]
    up_factor[...] = act * scale[...]
    hidden[...] = (h.astype(F32) * scale[...]).astype(BF)


def backward_kernel(
    where, ready, done, rows_grad, down_w, gate_factor, up_factor, gate_w, up_w,
    out, rows, d_gate, d_up
):
    blocks = rows_grad.shape[0]
    half = out.shape[2] // CORES
    ready(0)
    for b in range(blocks):
        rows[b * ROWS : (b + 1) * ROWS, :] = padded(rows_grad[b]).astype(BF)
    ready(1)
    d_hidden = dot(rows[...], down_w[...], 1, 1)
    ready(2, 3)
    dg = (d_hidden * gate_factor[...]).astype(BF)
    du = (d_hidden * up_factor[...]).astype(BF)
    ready(4, 5)
    for c in range(CORES):
        cols = slice(c * half, (c + 1) * half)
        piece = (dot(dg, gate_w[:, cols]) + dot(du, up_w[:, cols])).astype(BF)
        for d in range(blocks):
            out[d, :, cols] = piece[d * ROWS : d * ROWS + SLOTS]
    done(0)
    d_gate[...] = dg
    d_up[...] = du


def grads_kernel(
    where, ready, done, x, rows_grad, hidden, d_gate, d_up, g_gate, g_up, g_down
):
    ready(1, 2)
    g_down[...] = dot(hidden[...], rows_grad[...], 0, 0).astype(BF)
    done(2)
    ready(0, 3)
    g_gate[...] = dot(d_gate[...], x[...], 0, 0).astype(BF)
    done(0)
    ready(4)
    g_up[...] = dot(d_up[...], x[...], 0, 0).astype(BF)


def gathered(returned, total):
    sources = returned.shape[0]
    pieces = sources // EXP_DEV
    for j in range(EXP_DEV):
        part = None
        for d in range(j * pieces, (j + 1) * pieces):
            block = returned[d].astype(F32)
            part = block if part is None else part + block
        total[j * ROWS : (j + 1) * ROWS, :] = padded(part)
    return split(total[...])


def shared(core, full, keep, give):
    half = keep.shape[1]
    keep[...] = full[:, pl.ds(pl.multiple_of(core * half, LANES), half)]
    give[...] = full[:, pl.ds(pl.multiple_of((1 - core) * half, LANES), half)].astype(BF)


def combine_kernel(
    where, ready, done, returned, ids, weight, d_mixed, keep, give, route, place, total, full
):
    first_expert, core = where[0], where[1]
    rows = ids.shape[0]
    count = total.shape[0]
    lane = iota((rows, count), 1)
    expert = first_expert + lane // ROWS
    all_ids = ids[...]
    pick = rows_of_slots(all_ids, expert, lane % ROWS)
    place[...] = pick.astype(BF)
    scale = jnp.zeros((rows, count), F32)
    for k in range(ids.shape[1]):
        scale = scale + jnp.where(all_ids[:, k : k + 1] == expert, weight[:, k : k + 1], 0.0)
    high, low = split(pick * scale)
    ready(0)
    back, rest = gathered(returned, total)
    full[...] = dot(high, back) + (dot(low, back) + dot(high, rest))
    shared(core, full, keep, give)
    ready(3)
    grad = d_mixed[...]
    paired = (dot(grad, back, 1, 1) + dot(grad, rest, 1, 1)) * pick
    spot = iota((rows, LANES), 1)
    result = jnp.zeros((rows, LANES), F32)
    for k in range(ids.shape[1]):
        mine = jnp.where(all_ids[:, k : k + 1] == expert, paired, 0.0)
        result = jnp.where(spot % 8 == k, jnp.sum(mine, axis=1, keepdims=True), result)
    route[...] = result


def tokens_kernel(where, ready, done, returned, place, keep, give, total, full):
    back, rest = gathered(returned, total)
    full[...] = dot(place[...], back) + dot(place[...], rest)
    shared(where[0], full, keep, give)


def pack_kernel(
    where, ready, done, mixed, mixed_other, route, d_tokens, d_tokens_other, out
):
    half = mixed.shape[1]
    high, low = [part.astype(F32) for part in split(route[...])]
    sums = [mixed[...] + mixed_other[...].astype(F32)]
    sums.append(d_tokens[...] + d_tokens_other[...].astype(F32))
    for i in range(out.shape[0] // 2):
        rows = slice(8 * i, 8 * i + 8)
        for j, tail in enumerate((high, low)):
            out[2 * i + j, :, :half] = sums[j][rows].astype(BF)
            out[2 * i + j, :, half:] = tail[rows].astype(BF)


def total_kernel(where, ready, done, parts, out):
    total = parts[0].astype(F32)
    for i in range(1, parts.shape[0]):
        total = total + parts[i].astype(F32)
    width = total.shape[1] - LANES
    tail = total[:, width:]
    high, low = split(tail)
    spot = iota(tail.shape, 1)
    tail = jnp.where(spot < 8, high.astype(F32), low.astype(F32)).astype(BF)
    body_part = total[:, :width].astype(BF)
    for i in range(out.shape[0]):
        out[i, :, :width] = body_part
        out[i, :, width:] = tail


def finish_kernel(where, ready, done, own, other, mixed, d_tokens, route):
    core = where[0]
    width = own.shape[2] - LANES
    for source, side in ((own, core), (other, 1 - core)):
        cols = pl.ds(pl.multiple_of(side * width, LANES), width)
        for target, odd in ((mixed, 0), (d_tokens, 1)):
            for i in range(0, own.shape[0] // 2, 2):
                pair = [source[2 * (i + j) + odd, :, :width].astype(F32) for j in range(2)]
                target[8 * i : 8 * i + 16, cols] = jnp.concatenate(pair, axis=0).astype(BF)
    parts = []
    for i in range(own.shape[0] // 2):
        total = jnp.zeros((8, LANES), F32)
        for source in (own, other):
            for odd in range(2):
                total = total + source[2 * i + odd, :, width:].astype(F32)
        parts.append(total)
    total = jnp.concatenate(parts, axis=0).T
    count = route.shape[0]
    route[...] = total[:count] + total[8 : 8 + count]


def body(tokens, d_mixed, route_ids, route_weight, gate_weight, up_weight, down_weight):
    side = lax.axis_size("y")
    dp_count = lax.axis_size("x") * side
    z_count = lax.axis_size("z")
    z_index, core = lax.axis_index("z"), lax.axis_index("core")
    dp_index = lax.axis_index("x") * side + lax.axis_index("y")
    row_count, width = tokens.shape
    half = width // CORES
    hidden_count = gate_weight.shape[1]
    rows = dp_count * ROWS
    column_expert = (z_index * CORES + core) * EXP_DEV
    expert = column_expert + dp_index // (dp_count // EXP_DEV)
    gate_piece, up_piece, down_piece = gate_weight[0], up_weight[0], down_weight[0]
    out_shape = (dp_count, SLOTS, width)
    gathered_v = pltpu.VMEM((EXP_DEV * ROWS, width), F32)
    full_v = pltpu.VMEM((row_count, width), F32)

    def own_rows(array):
        return lax.dynamic_slice_in_dim(array, dp_index * row_count, row_count, 0)

    def send(array, ids):
        (sent,) = call(
            send_kernel,
            [((dp_count, SLOTS, width), BF, HBM)],
            [column_expert],
            [(ids, VMEM), (array, HBM)],
        )
        return sent

    ids, all_ids, all_weight = own_rows(route_ids).T, route_ids.T, route_weight.T
    shapes = [((dp_count, SLOTS, width), BF), ((rows, 1), F32)]
    experts = (column_expert, expert)
    prepared = prepare(0, core, experts, ids, d_mixed, all_ids, all_weight, shapes)
    *prepared, first_ids = lax.optimization_barrier((*prepared, ids))
    sent = send(tokens, first_ids)
    sent, ids, route_ids, route_weight = lax.optimization_barrier(
        (sent, ids, route_ids, route_weight)
    )
    rows_in = lax.all_to_all(sent, ("x", "y"), 0, 0, tiled=True)
    sent_grad, scale = prepare(
        1, core, experts, ids, d_mixed, all_ids, all_weight, shapes, prepared
    )
    rows_grad = lax.all_to_all(sent_grad, ("x", "y"), 0, 0, tiled=True)

    out, x, gate_factor, up_factor, hidden = call(
        forward_kernel,
        [
            (out_shape, BF, HBM),
            ((rows, width), BF, HBM),
            ((rows, hidden_count), F32, HBM),
            ((rows, hidden_count), F32, HBM),
            ((rows, hidden_count), BF, HBM),
        ],
        [expert],
        [
            (scale, HBM),
            (rows_in, VMEM),
            (gate_piece, HBM),
            (up_piece, HBM),
            (down_piece, HBM),
        ],
        vmem=24,
    )
    out, rows_grad = lax.optimization_barrier((out, rows_grad))
    returned = lax.all_to_all(out, ("x", "y"), 0, 0, tiled=True)

    out_in, padded_grad, d_gate, d_up = call(
        backward_kernel,
        [
            (out_shape, BF, HBM),
            ((rows, width), BF, HBM),
            ((rows, hidden_count), BF, HBM),
            ((rows, hidden_count), BF, HBM),
        ],
        [expert],
        [
            (rows_grad, HBM),
            (down_piece, HBM),
            (gate_factor, HBM),
            (up_factor, HBM),
            (gate_piece, HBM),
            (up_piece, HBM),
        ],
        vmem=24,
    )
    grads = call(
        grads_kernel,
        [((hidden_count, width), BF, HBM)] * 3,
        [expert],
        [(x, HBM), (padded_grad, HBM), (hidden, HBM), (d_gate, HBM), (d_up, HBM)],
        vmem=24,
    )
    grad_gate, grad_up, grad_down, out_in, route_ids, route_weight = lax.optimization_barrier(
        (*grads, out_in, route_ids, route_weight)
    )
    returned_in = lax.all_to_all(out_in, ("x", "y"), 0, 0, tiled=True)
    swap = [(0, 1), (1, 0)]
    shares = [((row_count, half), F32, VMEM), ((row_count, half), BF, VMEM)]
    mixed_part, mixed_give, route_part, own_place = call(
        combine_kernel,
        [
            *shares,
            ((row_count, LANES), F32, VMEM),
            ((row_count, EXP_DEV * ROWS), BF, VMEM),
        ],
        [column_expert, core],
        [
            (returned, VMEM),
            (own_rows(route_ids), VMEM),
            (own_rows(route_weight), VMEM),
            (d_mixed, HBM),
        ],
        [gathered_v, full_v],
        vmem=16,
    )
    mixed_other = lax.ppermute(mixed_give, "core", swap)
    tokens_part, tokens_give = call(
        tokens_kernel,
        shares,
        [core],
        [(returned_in, VMEM), (own_place, VMEM)],
        [gathered_v, full_v],
    )
    tokens_other = lax.ppermute(tokens_give, "core", swap)
    (packed,) = call(
        pack_kernel,
        [((z_count, 8, half + LANES), BF, VMEM)],
        [core],
        [
            (mixed_part, VMEM),
            (mixed_other, VMEM),
            (route_part, VMEM),
            (tokens_part, VMEM),
            (tokens_other, VMEM),
        ],
    )
    parts = lax.all_to_all(packed, "z", 0, 0, tiled=True)
    (summed,) = call(
        total_kernel, [((z_count, 8, half + LANES), BF, VMEM)], [core], [(parts, VMEM)]
    )
    whole = lax.all_to_all(summed, "z", 0, 0, tiled=True)
    other = lax.ppermute(whole, "core", swap)
    mixed, d_tokens, d_route = call(
        finish_kernel,
        [
            ((row_count, width), BF, VMEM),
            ((row_count, width), BF, VMEM),
            ((route_ids.shape[1], row_count), F32, VMEM),
        ],
        [core],
        [(whole, VMEM), (other, VMEM)],
    )
    return (mixed, d_route.T, d_tokens, grad_gate[None], grad_up[None], grad_down[None])


def solution(mesh):
    dp_count, expert_count = mesh.devices.shape
    side = math.isqrt(dp_count)
    fine = Mesh(
        mesh.devices.reshape(side, side, expert_count // CORES, CORES), ("x", "y", "z", "core")
    )
    rows = P(("x", "y"), None)
    blocks = P(("z", "core", "x", "y"), None, None)
    in_specs = (rows, rows, P(), P(), blocks, blocks, blocks)
    out_specs = (rows, rows, rows, blocks, blocks, blocks)
    return jax.shard_map(body, mesh=fine, in_specs=in_specs, out_specs=out_specs, check_vma=False)
```

```python
import math

import jax
import jax.numpy as jnp
from jax import lax
from jax.experimental import pallas as pl
from jax.experimental.pallas import tpu as pltpu
from jax.sharding import Mesh, PartitionSpec as P

CORES = 2
EXP_DEV = 2
SLOTS = 30
ROWS = 32
LANES = 128
BF = jnp.bfloat16
F32 = jnp.float32


def dot(left, right, left_dim=1, right_dim=0):
    return lax.dot_general(
        left, right, (((left_dim,), (right_dim,)), ((), ())), preferred_element_type=F32
    )


def iota(shape, dim):
    return lax.broadcasted_iota(jnp.int32, shape, dim)


def split(value):
    high = value.astype(BF)
    return high, (value - high.astype(F32)).astype(BF)


def slot_rows_of(ids, expert, slot, block):
    count = ids.shape[1]
    hit = ids[0:1, :] == expert
    for k in range(1, ids.shape[0]):
        hit = jnp.logical_or(hit, ids[k : k + 1, :] == expert)
    flag = hit.astype(F32)
    before, after = iota((count, count), 0), iota((count, count), 1)
    earlier = jnp.logical_and(before < after, before // block == after // block).astype(BF)
    return jnp.where(dot(flag.astype(BF), earlier) == slot.astype(F32), flag, 0.0)


def rows_of_slots(ids, expert, slot):
    count = ids.shape[0]
    hit = ids[:, 0:1] == expert
    for k in range(1, ids.shape[1]):
        hit = jnp.logical_or(hit, ids[:, k : k + 1] == expert)
    flag = hit.astype(F32)
    earlier = (iota((count, count), 1) < iota((count, count), 0)).astype(BF)
    return jnp.where(dot(earlier, flag.astype(BF)) == slot.astype(F32), flag, 0.0)


VMEM = pl.BlockSpec(memory_space=pltpu.VMEM)
HBM = pl.BlockSpec(memory_space=pltpu.HBM)


def begin(pairs, sems):
    copies = [pltpu.make_async_copy(a, b, sems.at[i]) for i, (a, b) in enumerate(pairs)]
    for copy in copies:
        copy.start()
    return copies


def call(kernel, outs, scalars, arrays, scratch=(), vmem=8):
    ins = [i for i, (_, space) in enumerate(arrays) if space is HBM]
    kept = [i for i, (_, _, space) in enumerate(outs) if space is HBM]
    count, total = len(arrays), len(arrays) + len(outs)

    def wrapped(where, *refs):
        given, results, rest = list(refs[:count]), list(refs[count:total]), list(refs[total:])
        in_sem, out_sem = rest.pop(), rest.pop()
        loads = {}
        for n, i in enumerate(ins):
            loads[i] = pltpu.make_async_copy(given[i], rest[n], in_sem.at[n])
            loads[i].start()
            given[i] = rest[n]
        rest = rest[len(ins) :]
        targets = {}
        for n, i in enumerate(kept):
            targets[i] = (results[i], out_sem.at[n])
            results[i] = rest[n]
        rest = rest[len(kept) :]
        stores = []

        def ready(*names):
            for i in names:
                if i in loads:
                    loads.pop(i).wait()

        def done(i):
            target, sem = targets.pop(i)
            stores.append(pltpu.make_async_copy(results[i], target, sem))
            stores[-1].start()

        kernel(where, ready, done, *given, *results, *rest)
        ready(*list(loads))
        for i in list(targets):
            done(i)
        for store in stores:
            store.wait()

    def held(array, space):
        return pltpu.with_memory_space_constraint(array, pltpu.HBM) if space is HBM else array

    def result(shape, kind, space):
        return pltpu.HBM(shape, kind) if space is HBM else jax.ShapeDtypeStruct(shape, kind)

    dma = pltpu.SemaphoreType.DMA
    return pl.pallas_call(
        wrapped,
        out_shape=[result(*out) for out in outs],
        in_specs=[pl.BlockSpec(memory_space=pltpu.SMEM)] + [space for _, space in arrays],
        out_specs=[space for _, _, space in outs],
        scratch_shapes=[pltpu.VMEM(arrays[i][0].shape, arrays[i][0].dtype) for i in ins]
        + [pltpu.VMEM(outs[i][0], outs[i][1]) for i in kept]
        + list(scratch)
        + [dma((max(1, len(kept)),)), dma((max(1, len(ins)),))],
        compiler_params=pltpu.CompilerParams(vmem_limit_bytes=vmem << 20),
    )(jnp.stack(scalars).astype(jnp.int32), *[held(*array) for array in arrays])


def padded(block):
    extra = jnp.zeros((ROWS - block.shape[0], block.shape[1]), F32)
    return jnp.concatenate([block.astype(F32), extra], axis=0)


def own_block(array, index, block):
    total = None
    for b in range(array.shape[1] // block):
        part = jnp.where(index == b, array[:, b * block : (b + 1) * block], 0)
        total = part if total is None else total + part
    return total


def send_kernel(where, ready, done, all_ids, tokens, out):
    block = tokens.shape[0]
    ready(0)
    ids = own_block(all_ids[...], where[1], block)
    spot = iota((EXP_DEV * ROWS, 1), 0)
    pick = slot_rows_of(ids, where[0] + spot // ROWS, spot % ROWS, block).astype(BF)
    ready(1)
    picked = dot(pick, tokens[...]).astype(BF)
    per_expert = out.shape[0] // EXP_DEV
    for d in range(out.shape[0]):
        first = d // per_expert * ROWS
        out[d] = picked[first : first + SLOTS]


def weights_of_slots(expert, ids, weight, block):
    slot = iota((ROWS, 1), 0)
    pick = slot_rows_of(ids, jnp.full((ROWS, 1), expert, jnp.int32), slot, block)
    scale = jnp.zeros((1, ids.shape[1]), F32)
    for k in range(ids.shape[0]):
        scale = scale + jnp.where(ids[k : k + 1, :] == expert, weight[k : k + 1, :], 0.0)
    scale = pick * scale
    owner = iota(scale.shape, 1) // block
    return [
        jnp.sum(jnp.where(owner == j, scale, 0.0), axis=1, keepdims=True)
        for j in range(ids.shape[1] // block)
    ]


def prepare_kernel(where, rows, all_ids, all_weight, *refs):
    out, scale, rows_v, ids_v, weight_v, picked, scale_v = refs[-7:]

    @pl.when(where[2] == where[3])
    def _():
        pltpu.sync_copy(rows, rows_v)
        pltpu.sync_copy(all_ids, ids_v)
        send_kernel(where, lambda _: None, None, ids_v, rows_v, picked)
        pltpu.sync_copy(picked, out)
        pltpu.sync_copy(all_weight, weight_v)
        block = rows.shape[0]
        per_step = LANES // block

        def some_blocks(i, carry):
            cols = pl.ds(pl.multiple_of(i * LANES, LANES), LANES)
            parts = weights_of_slots(where[4], ids_v[:, cols], weight_v[:, cols], block)
            for j, part in enumerate(parts):
                first = pl.multiple_of((i * per_step + j) * ROWS, ROWS)
                scale_v[pl.ds(first, ROWS), :] = part
            return carry

        lax.fori_loop(0, all_ids.shape[1] // LANES, some_blocks, 0)
        pltpu.sync_copy(scale_v, scale)


def prepare(turn, core, column_expert, dp_index, expert, rows, all_ids, all_weight, shapes, before=()):
    arrays = [
        pltpu.with_memory_space_constraint(array, pltpu.HBM)
        for array in (rows, all_ids, all_weight, *before)
    ]
    (out, out_kind), (scale, scale_kind) = shapes
    return pl.pallas_call(
        prepare_kernel,
        out_shape=[pltpu.HBM(out, out_kind), pltpu.HBM(scale, scale_kind)],
        in_specs=[pl.BlockSpec(memory_space=pltpu.SMEM)] + [HBM] * len(arrays),
        out_specs=[HBM, HBM],
        input_output_aliases={4: 0, 5: 1} if before else {},
        scratch_shapes=[
            pltpu.VMEM(rows.shape, rows.dtype),
            pltpu.VMEM(all_ids.shape, all_ids.dtype),
            pltpu.VMEM(all_weight.shape, all_weight.dtype),
            pltpu.VMEM(out, out_kind),
            pltpu.VMEM(scale, scale_kind),
        ],
        compiler_params=pltpu.CompilerParams(vmem_limit_bytes=8 << 20),
    )(
        jnp.stack([column_expert, dp_index, core, jnp.int32(turn), expert]).astype(jnp.int32),
        *arrays,
    )


def forward_kernel(
    where, ready, done, scale, rows_in, gate_w, up_w, down_w,
    out, x, gate_factor, up_factor, hidden
):
    blocks = rows_in.shape[0]
    half = out.shape[2] // CORES
    for b in range(blocks):
        x[b * ROWS : (b + 1) * ROWS, :] = padded(rows_in[b]).astype(BF)
    done(1)
    ready(2, 3)
    g = dot(x[...], gate_w[...], 1, 1)
    u = dot(x[...], up_w[...], 1, 1)
    sig = jax.nn.sigmoid(g)
    act = g * sig
    h = (act * u).astype(BF)
    ready(4)
    for c in range(CORES):
        cols = slice(c * half, (c + 1) * half)
        piece = dot(h, down_w[:, cols]).astype(BF)
        for d in range(blocks):
            out[d, :, cols] = piece[d * ROWS : d * ROWS + SLOTS]
    done(0)
    ready(0)
    gate_factor[...] = u * sig * (1.0 + g * (1.0 - sig)) * scale[...]
    up_factor[...] = act * scale[...]
    hidden[...] = (h.astype(F32) * scale[...]).astype(BF)


def backward_kernel(
    where, ready, done, rows_grad, down_w, gate_factor, up_factor, gate_w, up_w,
    out, rows, d_gate, d_up
):
    blocks = rows_grad.shape[0]
    half = out.shape[2] // CORES
    ready(0)
    for b in range(blocks):
        rows[b * ROWS : (b + 1) * ROWS, :] = padded(rows_grad[b]).astype(BF)
    ready(1)
    d_hidden = dot(rows[...], down_w[...], 1, 1)
    ready(2, 3)
    dg = (d_hidden * gate_factor[...]).astype(BF)
    du = (d_hidden * up_factor[...]).astype(BF)
    ready(4, 5)
    for c in range(CORES):
        cols = slice(c * half, (c + 1) * half)
        piece = (dot(dg, gate_w[:, cols]) + dot(du, up_w[:, cols])).astype(BF)
        for d in range(blocks):
            out[d, :, cols] = piece[d * ROWS : d * ROWS + SLOTS]
    done(0)
    d_gate[...] = dg
    d_up[...] = du


def grads_kernel(
    where, ready, done, x, rows_grad, hidden, d_gate, d_up, g_gate, g_up, g_down
):
    ready(1, 2)
    g_down[...] = dot(hidden[...], rows_grad[...], 0, 0).astype(BF)
    done(2)
    ready(0, 3)
    g_gate[...] = dot(d_gate[...], x[...], 0, 0).astype(BF)
    done(0)
    ready(4)
    g_up[...] = dot(d_up[...], x[...], 0, 0).astype(BF)


def gathered(returned, total):
    sources = returned.shape[0]
    pieces = sources // EXP_DEV
    for j in range(EXP_DEV):
        part = None
        for d in range(j * pieces, (j + 1) * pieces):
            block = returned[d].astype(F32)
            part = block if part is None else part + block
        total[j * ROWS : (j + 1) * ROWS, :] = padded(part)
    return split(total[...])


def shared(core, full, keep, give):
    half = keep.shape[1]
    keep[...] = full[:, pl.ds(pl.multiple_of(core * half, LANES), half)]
    give[...] = full[:, pl.ds(pl.multiple_of((1 - core) * half, LANES), half)].astype(BF)


def combine_kernel(
    where, ready, done, returned, ids, weight, d_mixed, keep, give, route, place, total, full
):
    first_expert, core = where[0], where[1]
    rows = ids.shape[0]
    count = total.shape[0]
    lane = iota((rows, count), 1)
    expert = first_expert + lane // ROWS
    all_ids = ids[...]
    pick = rows_of_slots(all_ids, expert, lane % ROWS)
    place[...] = pick.astype(BF)
    scale = jnp.zeros((rows, count), F32)
    for k in range(ids.shape[1]):
        scale = scale + jnp.where(all_ids[:, k : k + 1] == expert, weight[:, k : k + 1], 0.0)
    high, low = split(pick * scale)
    ready(0)
    back, rest = gathered(returned, total)
    full[...] = dot(high, back) + (dot(low, back) + dot(high, rest))
    shared(core, full, keep, give)
    ready(3)
    grad = d_mixed[...]
    paired = (dot(grad, back, 1, 1) + dot(grad, rest, 1, 1)) * pick
    spot = iota((rows, LANES), 1)
    result = jnp.zeros((rows, LANES), F32)
    for k in range(ids.shape[1]):
        mine = jnp.where(all_ids[:, k : k + 1] == expert, paired, 0.0)
        result = jnp.where(spot % 8 == k, jnp.sum(mine, axis=1, keepdims=True), result)
    route[...] = result


def tokens_kernel(where, returned, place, out, held, total, sems):
    width = out.shape[1]
    cols = pl.ds(pl.multiple_of(where[0] * width, LANES), width)
    pieces = held.shape[0] // EXP_DEV
    spans = [slice(j * pieces, (j + 1) * pieces) for j in range(EXP_DEV)]
    loads = begin([(returned.at[span, :, cols], held.at[span]) for span in spans], sems)
    for j, span in enumerate(spans):
        loads[j].wait()
        part = held[span.start].astype(F32)
        for d in range(span.start + 1, span.stop):
            part = part + held[d].astype(F32)
        total[j * ROWS : (j + 1) * ROWS, :] = padded(part)
    back, rest = split(total[...])
    out[...] = (dot(place[...], back) + dot(place[...], rest)).astype(out.dtype)


def tokens_half(side, returned, place, kind):
    sources, slots, width = returned.shape
    half = width // CORES
    return pl.pallas_call(
        tokens_kernel,
        out_shape=jax.ShapeDtypeStruct((place.shape[0], half), kind),
        in_specs=[pl.BlockSpec(memory_space=pltpu.SMEM), HBM, VMEM],
        out_specs=VMEM,
        scratch_shapes=[
            pltpu.VMEM((sources, slots, half), BF),
            pltpu.VMEM((EXP_DEV * ROWS, half), F32),
            pltpu.SemaphoreType.DMA((EXP_DEV,)),
        ],
        compiler_params=pltpu.CompilerParams(vmem_limit_bytes=8 << 20),
    )(side.reshape(1), pltpu.with_memory_space_constraint(returned, pltpu.HBM), place)


def pack_kernel(
    where, ready, done, mixed, mixed_other, route, d_tokens, d_tokens_other, out
):
    half = mixed.shape[1]
    high, low = [part.astype(F32) for part in split(route[...])]
    sums = [mixed[...] + mixed_other[...].astype(F32)]
    sums.append(d_tokens[...] + d_tokens_other[...].astype(F32))
    for i in range(out.shape[0] // 2):
        rows = slice(8 * i, 8 * i + 8)
        for j, tail in enumerate((high, low)):
            out[2 * i + j, :, :half] = sums[j][rows].astype(BF)
            out[2 * i + j, :, half:] = tail[rows].astype(BF)


def total_kernel(where, ready, done, parts, out):
    total = parts[0].astype(F32)
    for i in range(1, parts.shape[0]):
        total = total + parts[i].astype(F32)
    width = total.shape[1] - LANES
    tail = total[:, width:]
    high, low = split(tail)
    spot = iota(tail.shape, 1)
    tail = jnp.where(spot < 8, high.astype(F32), low.astype(F32)).astype(BF)
    body_part = total[:, :width].astype(BF)
    for i in range(out.shape[0]):
        out[i, :, :width] = body_part
        out[i, :, width:] = tail


def finish_kernel(where, ready, done, own, other, mixed, d_tokens, route):
    core = where[0]
    width = own.shape[2] - LANES
    for source, side in ((own, core), (other, 1 - core)):
        cols = pl.ds(pl.multiple_of(side * width, LANES), width)
        for target, odd in ((mixed, 0), (d_tokens, 1)):
            for i in range(0, own.shape[0] // 2, 2):
                pair = [source[2 * (i + j) + odd, :, :width].astype(F32) for j in range(2)]
                target[8 * i : 8 * i + 16, cols] = jnp.concatenate(pair, axis=0).astype(BF)
    parts = []
    for i in range(own.shape[0] // 2):
        total = jnp.zeros((8, LANES), F32)
        for source in (own, other):
            for odd in range(2):
                total = total + source[2 * i + odd, :, width:].astype(F32)
        parts.append(total)
    total = jnp.concatenate(parts, axis=0).T
    count = route.shape[0]
    route[...] = total[:count] + total[8 : 8 + count]


def body(tokens, d_mixed, route_ids, route_weight, gate_weight, up_weight, down_weight):
    side = lax.axis_size("y")
    dp_count = lax.axis_size("x") * side
    z_count = lax.axis_size("z")
    z_index, core = lax.axis_index("z"), lax.axis_index("core")
    dp_index = lax.axis_index("x") * side + lax.axis_index("y")
    row_count, width = tokens.shape
    half = width // CORES
    hidden_count = gate_weight.shape[1]
    rows = dp_count * ROWS
    column_expert = (z_index * CORES + core) * EXP_DEV
    expert = column_expert + dp_index // (dp_count // EXP_DEV)
    gate_piece, up_piece, down_piece = gate_weight[0], up_weight[0], down_weight[0]
    out_shape = (dp_count, SLOTS, width)
    gathered_v = pltpu.VMEM((EXP_DEV * ROWS, width), F32)
    full_v = pltpu.VMEM((row_count, width), F32)

    def own_rows(array):
        return lax.dynamic_slice_in_dim(array, dp_index * row_count, row_count, 0)

    all_ids, all_weight = route_ids.T, route_weight.T
    shapes = [((dp_count, SLOTS, width), BF), ((rows, 1), F32)]
    prepare_in = (core, column_expert, dp_index, expert, d_mixed, all_ids, all_weight, shapes)
    prepared = prepare(0, *prepare_in)
    *prepared, first_ids = lax.optimization_barrier((*prepared, all_ids))
    (sent,) = call(
        send_kernel,
        [((dp_count, SLOTS, width), BF, HBM)],
        [column_expert, dp_index],
        [(first_ids, HBM), (tokens, HBM)],
    )
    sent, route_ids, route_weight, *prepared = lax.optimization_barrier(
        (sent, route_ids, route_weight, *prepared)
    )
    rows_in = lax.all_to_all(sent, ("x", "y"), 0, 0, tiled=True)
    sent_grad, scale = prepare(1, *prepare_in, prepared)
    rows_grad = lax.all_to_all(sent_grad, ("x", "y"), 0, 0, tiled=True)

    out, x, gate_factor, up_factor, hidden = call(
        forward_kernel,
        [
            (out_shape, BF, HBM),
            ((rows, width), BF, HBM),
            ((rows, hidden_count), F32, HBM),
            ((rows, hidden_count), F32, HBM),
            ((rows, hidden_count), BF, HBM),
        ],
        [expert],
        [
            (scale, HBM),
            (rows_in, VMEM),
            (gate_piece, HBM),
            (up_piece, HBM),
            (down_piece, HBM),
        ],
        vmem=24,
    )
    out, rows_grad = lax.optimization_barrier((out, rows_grad))
    returned = lax.all_to_all(out, ("x", "y"), 0, 0, tiled=True)

    out_in, padded_grad, d_gate, d_up = call(
        backward_kernel,
        [
            (out_shape, BF, HBM),
            ((rows, width), BF, HBM),
            ((rows, hidden_count), BF, HBM),
            ((rows, hidden_count), BF, HBM),
        ],
        [expert],
        [
            (rows_grad, HBM),
            (down_piece, HBM),
            (gate_factor, HBM),
            (up_factor, HBM),
            (gate_piece, HBM),
            (up_piece, HBM),
        ],
        vmem=24,
    )
    grads = call(
        grads_kernel,
        [((hidden_count, width), BF, HBM)] * 3,
        [expert],
        [(x, HBM), (padded_grad, HBM), (hidden, HBM), (d_gate, HBM), (d_up, HBM)],
        vmem=24,
    )
    grad_gate, grad_up, grad_down, out_in, route_ids, route_weight = lax.optimization_barrier(
        (*grads, out_in, route_ids, route_weight)
    )
    returned_in = lax.all_to_all(out_in, ("x", "y"), 0, 0, tiled=True)
    swap = [(0, 1), (1, 0)]
    shares = [((row_count, half), F32, VMEM), ((row_count, half), BF, VMEM)]
    mixed_part, mixed_give, route_part, own_place = call(
        combine_kernel,
        [
            *shares,
            ((row_count, LANES), F32, VMEM),
            ((row_count, EXP_DEV * ROWS), BF, VMEM),
        ],
        [column_expert, core],
        [
            (returned, VMEM),
            (own_rows(route_ids), VMEM),
            (own_rows(route_weight), VMEM),
            (d_mixed, HBM),
        ],
        [gathered_v, full_v],
    )
    mixed_other = lax.ppermute(mixed_give, "core", swap)
    tokens_give = tokens_half(1 - core, returned_in, own_place, BF)
    tokens_other = lax.ppermute(tokens_give, "core", swap)
    returned_in, tokens_give = lax.optimization_barrier((returned_in, tokens_give))
    tokens_part = tokens_half(core, returned_in, own_place, F32)
    (packed,) = call(
        pack_kernel,
        [((z_count, 8, half + LANES), BF, VMEM)],
        [core],
        [
            (mixed_part, VMEM),
            (mixed_other, VMEM),
            (route_part, VMEM),
            (tokens_part, VMEM),
            (tokens_other, VMEM),
        ],
    )
    parts = lax.all_to_all(packed, "z", 0, 0, tiled=True)
    (summed,) = call(
        total_kernel, [((z_count, 8, half + LANES), BF, VMEM)], [core], [(parts, VMEM)]
    )
    whole = lax.all_to_all(summed, "z", 0, 0, tiled=True)
    other = lax.ppermute(whole, "core", swap)
    mixed, d_tokens, d_route = call(
        finish_kernel,
        [
            ((row_count, width), BF, VMEM),
            ((row_count, width), BF, VMEM),
            ((route_ids.shape[1], row_count), F32, VMEM),
        ],
        [core],
        [(whole, VMEM), (other, VMEM)],
    )
    return (mixed, d_route.T, d_tokens, grad_gate[None], grad_up[None], grad_down[None])


def solution(mesh):
    dp_count, expert_count = mesh.devices.shape
    side = math.isqrt(dp_count)
    fine = Mesh(
        mesh.devices.reshape(side, side, expert_count // CORES, CORES), ("x", "y", "z", "core")
    )
    rows = P(("x", "y"), None)
    blocks = P(("z", "core", "x", "y"), None, None)
    in_specs = (rows, rows, P(), P(), blocks, blocks, blocks)
    out_specs = (rows, rows, rows, blocks, blocks, blocks)
    return jax.shard_map(body, mesh=fine, in_specs=in_specs, out_specs=out_specs, check_vma=False)
```

```python
import math

import jax
import jax.numpy as jnp
from jax import lax
from jax.experimental import pallas as pl
from jax.experimental.pallas import tpu as pltpu
from jax.sharding import Mesh, PartitionSpec as P

CORES = 2
EXP_DEV = 2
SLOTS = 30
ROWS = 32
LANES = 128
BF = jnp.bfloat16
F32 = jnp.float32


def dot(left, right, left_dim=1, right_dim=0):
    return lax.dot_general(
        left, right, (((left_dim,), (right_dim,)), ((), ())), preferred_element_type=F32
    )


def iota(shape, dim):
    return lax.broadcasted_iota(jnp.int32, shape, dim)


def split(value):
    high = value.astype(BF)
    return high, (value - high.astype(F32)).astype(BF)


def slot_rows_of(ids, expert, slot, block):
    count = ids.shape[1]
    hit = ids[0:1, :] == expert
    for k in range(1, ids.shape[0]):
        hit = jnp.logical_or(hit, ids[k : k + 1, :] == expert)
    flag = hit.astype(F32)
    before, after = iota((count, count), 0), iota((count, count), 1)
    earlier = jnp.logical_and(before < after, before // block == after // block).astype(BF)
    return jnp.where(dot(flag.astype(BF), earlier) == slot.astype(F32), flag, 0.0)


def rows_of_slots(ids, expert, slot):
    count = ids.shape[0]
    hit = ids[:, 0:1] == expert
    for k in range(1, ids.shape[1]):
        hit = jnp.logical_or(hit, ids[:, k : k + 1] == expert)
    flag = hit.astype(F32)
    earlier = (iota((count, count), 1) < iota((count, count), 0)).astype(BF)
    return jnp.where(dot(earlier, flag.astype(BF)) == slot.astype(F32), flag, 0.0)


VMEM = pl.BlockSpec(memory_space=pltpu.VMEM)
HBM = pl.BlockSpec(memory_space=pltpu.HBM)


def begin(pairs, sems):
    copies = [pltpu.make_async_copy(a, b, sems.at[i]) for i, (a, b) in enumerate(pairs)]
    for copy in copies:
        copy.start()
    return copies


def call(kernel, outs, scalars, arrays, scratch=(), vmem=8):
    ins = [i for i, (_, space) in enumerate(arrays) if space is HBM]
    kept = [i for i, (_, _, space) in enumerate(outs) if space is HBM]
    count, total = len(arrays), len(arrays) + len(outs)

    def wrapped(where, *refs):
        given, results, rest = list(refs[:count]), list(refs[count:total]), list(refs[total:])
        in_sem, out_sem = rest.pop(), rest.pop()
        loads = {}
        for n, i in enumerate(ins):
            loads[i] = pltpu.make_async_copy(given[i], rest[n], in_sem.at[n])
            loads[i].start()
            given[i] = rest[n]
        rest = rest[len(ins) :]
        targets = {}
        for n, i in enumerate(kept):
            targets[i] = (results[i], out_sem.at[n])
            results[i] = rest[n]
        rest = rest[len(kept) :]
        stores = []

        def ready(*names):
            for i in names:
                if i in loads:
                    loads.pop(i).wait()

        def done(i):
            target, sem = targets.pop(i)
            stores.append(pltpu.make_async_copy(results[i], target, sem))
            stores[-1].start()

        kernel(where, ready, done, *given, *results, *rest)
        ready(*list(loads))
        for i in list(targets):
            done(i)
        for store in stores:
            store.wait()

    def held(array, space):
        return pltpu.with_memory_space_constraint(array, pltpu.HBM) if space is HBM else array

    def result(shape, kind, space):
        return pltpu.HBM(shape, kind) if space is HBM else jax.ShapeDtypeStruct(shape, kind)

    dma = pltpu.SemaphoreType.DMA
    return pl.pallas_call(
        wrapped,
        out_shape=[result(*out) for out in outs],
        in_specs=[pl.BlockSpec(memory_space=pltpu.SMEM)] + [space for _, space in arrays],
        out_specs=[space for _, _, space in outs],
        scratch_shapes=[pltpu.VMEM(arrays[i][0].shape, arrays[i][0].dtype) for i in ins]
        + [pltpu.VMEM(outs[i][0], outs[i][1]) for i in kept]
        + list(scratch)
        + [dma((max(1, len(kept)),)), dma((max(1, len(ins)),))],
        compiler_params=pltpu.CompilerParams(vmem_limit_bytes=vmem << 20),
    )(jnp.stack(scalars).astype(jnp.int32), *[held(*array) for array in arrays])


def padded(block):
    extra = jnp.zeros((ROWS - block.shape[0], block.shape[1]), F32)
    return jnp.concatenate([block.astype(F32), extra], axis=0)


def send_kernel(where, ready, done, ids, tokens, out):
    spot = iota((EXP_DEV * ROWS, 1), 0)
    pick = slot_rows_of(ids[...], where[0] + spot // ROWS, spot % ROWS, ids.shape[1]).astype(BF)
    ready(1)
    picked = dot(pick, tokens[...]).astype(BF)
    per_expert = out.shape[0] // EXP_DEV
    for d in range(out.shape[0]):
        first = d // per_expert * ROWS
        out[d] = picked[first : first + SLOTS]


def weights_of_slots(expert, ids, weight, block):
    slot = iota((ROWS, 1), 0)
    pick = slot_rows_of(ids, jnp.full((ROWS, 1), expert, jnp.int32), slot, block)
    scale = jnp.zeros((1, ids.shape[1]), F32)
    for k in range(ids.shape[0]):
        scale = scale + jnp.where(ids[k : k + 1, :] == expert, weight[k : k + 1, :], 0.0)
    scale = pick * scale
    owner = iota(scale.shape, 1) // block
    return [
        jnp.sum(jnp.where(owner == j, scale, 0.0), axis=1, keepdims=True)
        for j in range(ids.shape[1] // block)
    ]


def prepare_kernel(where, ids, rows, all_ids, all_weight, *refs):
    out, scale, rows_v, ids_v, weight_v, picked, scale_v = refs[-7:]

    @pl.when(where[1] == where[2])
    def _():
        pltpu.sync_copy(rows, rows_v)
        send_kernel(where, lambda _: None, None, ids, rows_v, picked)
        pltpu.sync_copy(picked, out)
        pltpu.sync_copy(all_ids, ids_v)
        pltpu.sync_copy(all_weight, weight_v)
        block = ids.shape[1]
        per_step = LANES // block

        def some_blocks(i, carry):
            cols = pl.ds(pl.multiple_of(i * LANES, LANES), LANES)
            parts = weights_of_slots(where[3], ids_v[:, cols], weight_v[:, cols], block)
            for j, part in enumerate(parts):
                first = pl.multiple_of((i * per_step + j) * ROWS, ROWS)
                scale_v[pl.ds(first, ROWS), :] = part
            return carry

        lax.fori_loop(0, all_ids.shape[1] // LANES, some_blocks, 0)
        pltpu.sync_copy(scale_v, scale)


def prepare(turn, core, experts, ids, rows, all_ids, all_weight, shapes, before=()):
    arrays = [
        pltpu.with_memory_space_constraint(array, pltpu.HBM)
        for array in (rows, all_ids, all_weight, *before)
    ]
    (out, out_kind), (scale, scale_kind) = shapes
    return pl.pallas_call(
        prepare_kernel,
        out_shape=[pltpu.HBM(out, out_kind), pltpu.HBM(scale, scale_kind)],
        in_specs=[pl.BlockSpec(memory_space=pltpu.SMEM), VMEM] + [HBM] * len(arrays),
        out_specs=[HBM, HBM],
        input_output_aliases={5: 0, 6: 1} if before else {},
        scratch_shapes=[
            pltpu.VMEM(rows.shape, rows.dtype),
            pltpu.VMEM(all_ids.shape, all_ids.dtype),
            pltpu.VMEM(all_weight.shape, all_weight.dtype),
            pltpu.VMEM(out, out_kind),
            pltpu.VMEM(scale, scale_kind),
        ],
        compiler_params=pltpu.CompilerParams(vmem_limit_bytes=8 << 20),
    )(jnp.stack([experts[0], core, jnp.int32(turn), experts[1]]).astype(jnp.int32), ids, *arrays)


def forward_kernel(
    where, ready, done, scale, rows_in, gate_w, up_w, down_w,
    out, x, gate_factor, up_factor, hidden
):
    blocks = rows_in.shape[0]
    half = out.shape[2] // CORES
    for b in range(blocks):
        x[b * ROWS : (b + 1) * ROWS, :] = padded(rows_in[b]).astype(BF)
    done(1)
    ready(2, 3)
    g = dot(x[...], gate_w[...], 1, 1)
    u = dot(x[...], up_w[...], 1, 1)
    sig = jax.nn.sigmoid(g)
    act = g * sig
    h = (act * u).astype(BF)
    ready(4)
    for c in range(CORES):
        cols = slice(c * half, (c + 1) * half)
        piece = dot(h, down_w[:, cols]).astype(BF)
        for d in range(blocks):
            out[d, :, cols] = piece[d * ROWS : d * ROWS + SLOTS]
    done(0)
    ready(0)
    gate_factor[...] = u * sig * (1.0 + g * (1.0 - sig)) * scale[...]
    up_factor[...] = act * scale[...]
    hidden[...] = (h.astype(F32) * scale[...]).astype(BF)


def backward_kernel(
    where, ready, done, rows_grad, down_w, gate_factor, up_factor, gate_w, up_w,
    out, rows, d_gate, d_up
):
    blocks = rows_grad.shape[0]
    half = out.shape[2] // CORES
    ready(0)
    for b in range(blocks):
        rows[b * ROWS : (b + 1) * ROWS, :] = padded(rows_grad[b]).astype(BF)
    ready(1)
    d_hidden = dot(rows[...], down_w[...], 1, 1)
    ready(2, 3)
    dg = (d_hidden * gate_factor[...]).astype(BF)
    du = (d_hidden * up_factor[...]).astype(BF)
    ready(4, 5)
    for c in range(CORES):
        cols = slice(c * half, (c + 1) * half)
        piece = (dot(dg, gate_w[:, cols]) + dot(du, up_w[:, cols])).astype(BF)
        for d in range(blocks):
            out[d, :, cols] = piece[d * ROWS : d * ROWS + SLOTS]
    done(0)
    d_gate[...] = dg
    d_up[...] = du


def grads_kernel(
    where, ready, done, x, rows_grad, hidden, d_gate, d_up, g_gate, g_up, g_down
):
    ready(1, 2)
    g_down[...] = dot(hidden[...], rows_grad[...], 0, 0).astype(BF)
    done(2)
    ready(0, 3)
    g_gate[...] = dot(d_gate[...], x[...], 0, 0).astype(BF)
    done(0)
    ready(4)
    g_up[...] = dot(d_up[...], x[...], 0, 0).astype(BF)


def gathered(returned, total):
    sources = returned.shape[0]
    pieces = sources // EXP_DEV
    for j in range(EXP_DEV):
        part = None
        for d in range(j * pieces, (j + 1) * pieces):
            block = returned[d].astype(F32)
            part = block if part is None else part + block
        total[j * ROWS : (j + 1) * ROWS, :] = padded(part)
    return split(total[...])


def combine_kernel(
    where, ready, done, returned, ids, weight, d_mixed, keep, give, route, place, total
):
    first_expert = where[0]
    rows = ids.shape[0]
    count = total.shape[0]
    lane = iota((rows, count), 1)
    expert = first_expert + lane // ROWS
    all_ids = ids[...]
    pick = rows_of_slots(all_ids, expert, lane % ROWS)
    place[...] = pick.astype(BF)
    scale = jnp.zeros((rows, count), F32)
    for k in range(ids.shape[1]):
        scale = scale + jnp.where(all_ids[:, k : k + 1] == expert, weight[:, k : k + 1], 0.0)
    high, low = split(pick * scale)
    ready(0)
    back, rest = gathered(returned, total)
    keep[...] = dot(high, back) + (dot(low, back) + dot(high, rest))
    give[...] = keep[...].astype(BF)
    ready(3)
    grad = d_mixed[...]
    paired = (dot(grad, back, 1, 1) + dot(grad, rest, 1, 1)) * pick
    spot = iota((rows, LANES), 1)
    result = jnp.zeros((rows, LANES), F32)
    for k in range(ids.shape[1]):
        mine = jnp.where(all_ids[:, k : k + 1] == expert, paired, 0.0)
        result = jnp.where(spot % 8 == k, jnp.sum(mine, axis=1, keepdims=True), result)
    route[...] = result


def tokens_kernel(where, ready, done, returned, place, keep, give, total):
    back, rest = gathered(returned, total)
    keep[...] = dot(place[...], back) + dot(place[...], rest)
    give[...] = keep[...].astype(BF)


def pack_kernel(
    where, ready, done, mixed, mixed_other, route, d_tokens, d_tokens_other, out
):
    half = mixed.shape[1] // 2
    high, low = [part.astype(F32) for part in split(route[...])]
    sums = jnp.where(
        where[0] == 1,
        mixed[...] + mixed_other[...].astype(F32),
        d_tokens[...] + d_tokens_other[...].astype(F32),
    )
    for i in range(out.shape[0] // 2):
        rows = slice(8 * i, 8 * i + 8)
        for j, tail in enumerate((high, low)):
            out[2 * i + j, :, :half] = sums[rows, j * half : (j + 1) * half].astype(BF)
            out[2 * i + j, :, half:] = tail[rows].astype(BF)


def total_kernel(where, ready, done, parts, out):
    total = parts[0].astype(F32)
    for i in range(1, parts.shape[0]):
        total = total + parts[i].astype(F32)
    width = total.shape[1] - LANES
    tail = total[:, width:]
    high, low = split(tail)
    spot = iota(tail.shape, 1)
    tail = jnp.where(spot < 8, high.astype(F32), low.astype(F32)).astype(BF)
    body_part = total[:, :width].astype(BF)
    for i in range(out.shape[0]):
        out[i, :, :width] = body_part
        out[i, :, width:] = tail


def finish_kernel(where, ready, done, own, other, mixed, d_tokens, route):
    width = own.shape[2] - LANES
    mine = where[0] == 1
    for i in range(0, own.shape[0] // 2, 2):
        for j in range(2):
            cols = slice(j * width, (j + 1) * width)
            pairs = [
                jnp.concatenate(
                    [source[2 * (i + k) + j, :, :width].astype(F32) for k in range(2)], axis=0
                )
                for source in (own, other)
            ]
            mixed[8 * i : 8 * i + 16, cols] = jnp.where(mine, pairs[0], pairs[1]).astype(BF)
            d_tokens[8 * i : 8 * i + 16, cols] = jnp.where(mine, pairs[1], pairs[0]).astype(BF)
    parts = []
    for i in range(own.shape[0] // 2):
        total = jnp.zeros((8, LANES), F32)
        for source in (own, other):
            for j in range(2):
                total = total + source[2 * i + j, :, width:].astype(F32)
        parts.append(total)
    total = jnp.concatenate(parts, axis=0).T
    count = route.shape[0]
    route[...] = total[:count] + total[8 : 8 + count]


def body(tokens, d_mixed, route_ids, route_weight, gate_weight, up_weight, down_weight):
    side = lax.axis_size("y")
    dp_count = lax.axis_size("x") * side
    z_count = lax.axis_size("z")
    z_index, core = lax.axis_index("z"), lax.axis_index("core")
    dp_index = lax.axis_index("x") * side + lax.axis_index("y")
    row_count, width = tokens.shape
    half = width // CORES
    hidden_count = gate_weight.shape[1]
    rows = dp_count * ROWS
    column_expert = (z_index * CORES + core) * EXP_DEV
    expert = column_expert + dp_index // (dp_count // EXP_DEV)
    gate_piece, up_piece, down_piece = gate_weight[0], up_weight[0], down_weight[0]
    out_shape = (dp_count, SLOTS, width)
    gathered_v = pltpu.VMEM((EXP_DEV * ROWS, width), F32)

    def own_rows(array):
        return lax.dynamic_slice_in_dim(array, dp_index * row_count, row_count, 0)

    def send(array, ids):
        (sent,) = call(
            send_kernel,
            [((dp_count, SLOTS, width), BF, HBM)],
            [column_expert],
            [(ids, VMEM), (array, HBM)],
        )
        return sent

    ids, all_ids, all_weight = own_rows(route_ids).T, route_ids.T, route_weight.T
    shapes = [((dp_count, SLOTS, width), BF), ((rows, 1), F32)]
    experts = (column_expert, expert)
    prepared = prepare(0, core, experts, ids, d_mixed, all_ids, all_weight, shapes)
    *prepared, first_ids = lax.optimization_barrier((*prepared, ids))
    sent = send(tokens, first_ids)
    sent, ids, route_ids, route_weight = lax.optimization_barrier(
        (sent, ids, route_ids, route_weight)
    )
    rows_in = lax.all_to_all(sent, ("x", "y"), 0, 0, tiled=True)
    sent_grad, scale = prepare(
        1, core, experts, ids, d_mixed, all_ids, all_weight, shapes, prepared
    )
    rows_grad = lax.all_to_all(sent_grad, ("x", "y"), 0, 0, tiled=True)

    out, x, gate_factor, up_factor, hidden = call(
        forward_kernel,
        [
            (out_shape, BF, HBM),
            ((rows, width), BF, HBM),
            ((rows, hidden_count), F32, HBM),
            ((rows, hidden_count), F32, HBM),
            ((rows, hidden_count), BF, HBM),
        ],
        [expert],
        [
            (scale, HBM),
            (rows_in, VMEM),
            (gate_piece, HBM),
            (up_piece, HBM),
            (down_piece, HBM),
        ],
        vmem=24,
    )
    out, rows_grad = lax.optimization_barrier((out, rows_grad))
    returned = lax.all_to_all(out, ("x", "y"), 0, 0, tiled=True)

    out_in, padded_grad, d_gate, d_up = call(
        backward_kernel,
        [
            (out_shape, BF, HBM),
            ((rows, width), BF, HBM),
            ((rows, hidden_count), BF, HBM),
            ((rows, hidden_count), BF, HBM),
        ],
        [expert],
        [
            (rows_grad, HBM),
            (down_piece, HBM),
            (gate_factor, HBM),
            (up_factor, HBM),
            (gate_piece, HBM),
            (up_piece, HBM),
        ],
        vmem=24,
    )
    grads = call(
        grads_kernel,
        [((hidden_count, width), BF, HBM)] * 3,
        [expert],
        [(x, HBM), (padded_grad, HBM), (hidden, HBM), (d_gate, HBM), (d_up, HBM)],
        vmem=24,
    )
    grad_gate, grad_up, grad_down, out_in, route_ids, route_weight = lax.optimization_barrier(
        (*grads, out_in, route_ids, route_weight)
    )
    returned_in = lax.all_to_all(out_in, ("x", "y"), 0, 0, tiled=True)
    shares = [((row_count, width), F32, VMEM), ((row_count, width), BF, VMEM)]
    mixed_part, mixed_give, route_part, own_place = call(
        combine_kernel,
        [
            *shares,
            ((row_count, LANES), F32, VMEM),
            ((row_count, EXP_DEV * ROWS), BF, VMEM),
        ],
        [column_expert, core],
        [
            (returned, VMEM),
            (own_rows(route_ids), VMEM),
            (own_rows(route_weight), VMEM),
            (d_mixed, HBM),
        ],
        [gathered_v],
    )
    mixed_other = lax.ppermute(mixed_give, "core", [(0, 1)])
    tokens_part, tokens_give = call(
        tokens_kernel,
        shares,
        [core],
        [(returned_in, VMEM), (own_place, VMEM)],
        [gathered_v],
    )
    tokens_other = lax.ppermute(tokens_give, "core", [(1, 0)])
    (packed,) = call(
        pack_kernel,
        [((z_count, 8, half + LANES), BF, VMEM)],
        [core],
        [
            (mixed_part, VMEM),
            (mixed_other, VMEM),
            (route_part, VMEM),
            (tokens_part, VMEM),
            (tokens_other, VMEM),
        ],
    )
    parts = lax.all_to_all(packed, "z", 0, 0, tiled=True)
    (summed,) = call(
        total_kernel, [((z_count, 8, half + LANES), BF, VMEM)], [core], [(parts, VMEM)]
    )
    whole = lax.all_to_all(summed, "z", 0, 0, tiled=True)
    other = lax.ppermute(whole, "core", [(0, 1), (1, 0)])
    mixed, d_tokens, d_route = call(
        finish_kernel,
        [
            ((row_count, width), BF, VMEM),
            ((row_count, width), BF, VMEM),
            ((route_ids.shape[1], row_count), F32, VMEM),
        ],
        [core],
        [(whole, VMEM), (other, VMEM)],
    )
    return (mixed, d_route.T, d_tokens, grad_gate[None], grad_up[None], grad_down[None])


def solution(mesh):
    dp_count, expert_count = mesh.devices.shape
    side = math.isqrt(dp_count)
    fine = Mesh(
        mesh.devices.reshape(side, side, expert_count // CORES, CORES), ("x", "y", "z", "core")
    )
    rows = P(("x", "y"), None)
    blocks = P(("z", "core", "x", "y"), None, None)
    in_specs = (rows, rows, P(), P(), blocks, blocks, blocks)
    out_specs = (rows, rows, rows, blocks, blocks, blocks)
    return jax.shard_map(body, mesh=fine, in_specs=in_specs, out_specs=out_specs, check_vma=False)
```
